128 devices in a mesh: ctx: 16 (over y, x), head: 8 (over z, core).
Axes of the slice: x: 4, y: 4, z: 4, core: 2. Of those that a mesh axis runs over, the one named last changes fastest.
Arguments:
- input_queries: bfloat16 [16384, 6144], P(('ctx', 'head')), may hold values from -6 to 6
- input_keys: bfloat16 [16384, 1024], P(('ctx', 'head')), may hold values from -6 to 6
- input_values: bfloat16 [16384, 1024], P(('ctx', 'head')), may hold values from -6 to 6
- cotangent: bfloat16 [16384, 6144], P(('ctx', 'head')), may hold values from -6 to 6
- block_list: int32 [32, 8], replicated, may hold values from 0 to 31, as said below
- block_count: int32 [32], replicated, may hold values from 1 to 8, as said below
Outputs:
- attn_out: bfloat16 [16384, 6144], P(('ctx', 'head'))
- grad_query: bfloat16 [16384, 6144], P(('ctx', 'head'))
- key_gradient: bfloat16 [16384, 1024], P(('ctx', 'head'))
- value_gradient: bfloat16 [16384, 1024], P(('ctx', 'head'))
The draws below stay inside these ranges and needn't reach their ends.
Inputs may be any that keep to these rules, and one draw needn't show every extreme that they name: `block_list`: row b lists entry 0 = b itself, then distinct blocks of other ctx indices up to position block_count[b] - 1, block c belonging to ctx index c // 2; entries from position block_count[b] on repeat b and are unused. The rows of the 2 query blocks of one ctx index together name at most one block of any other ctx index. `block_count`: query block 0 lists 8 blocks.
All inputs are finite; a program needn't handle non-finite values.
Results may differ from the reference program's by a relative error of at most 0.015.
Values may be sent and summed in bfloat16 or wider, within the bound.
A program may use at most 128 MiB of HBM per device.

```python
import jax
import jax.numpy as jnp
from jax import lax

QUERY_HEADS = 48
KEY_VALUE_HEADS = 8
HEAD_WIDTH = 128
BLOCK_TOKENS = 512
MOST_KEY_BLOCKS = 8
QBLK_DEV = 2
SEQUENCE_BLOCKS = 32
SEQUENCE_TOKENS = 16384


def draw_input_keys(key, part):
    return jax.random.truncated_normal(jax.random.fold_in(key, 21), -6.0, 6.0, (SEQUENCE_TOKENS, KEY_VALUE_HEADS * HEAD_WIDTH), jnp.float32).astype(jnp.bfloat16)


def draw_input_queries(key, part):
    return jax.random.truncated_normal(jax.random.fold_in(key, 22), -6.0, 6.0, (SEQUENCE_TOKENS, QUERY_HEADS * HEAD_WIDTH), jnp.float32).astype(jnp.bfloat16)


def plan_lists(key):
    starting_key = jax.random.fold_in(key, 505)
    owner_total = SEQUENCE_BLOCKS // QBLK_DEV
    device_of = jnp.arange(SEQUENCE_BLOCKS) // QBLK_DEV
    load_level = jax.random.randint(jax.random.fold_in(starting_key, 1), (owner_total,), 0, 4)
    extra_span = 1 + 3 * load_level[device_of]
    extra_blocks = jnp.minimum(jax.random.randint(jax.random.fold_in(starting_key, 2), (SEQUENCE_BLOCKS,), 0, 2520) % extra_span, MOST_KEY_BLOCKS - 1)
    extra_blocks = extra_blocks.at[0].set(MOST_KEY_BLOCKS - 1)
    live_count = (1 + extra_blocks).astype(jnp.int32)
    chosen = jnp.arange(owner_total)[None, :] * QBLK_DEV + jax.random.randint(jax.random.fold_in(starting_key, 3), (owner_total, owner_total), 0, QBLK_DEV)
    order_key = jax.random.randint(jax.random.fold_in(starting_key, 4), (SEQUENCE_BLOCKS, owner_total), 0, 1 << 20) * owner_total + jnp.arange(owner_total)[None, :]
    order_key = jnp.where(jnp.arange(owner_total)[None, :] == device_of[:, None], 1 << 30, order_key)
    owner_order = jnp.argsort(order_key, axis=1)
    remote = owner_order[:, :MOST_KEY_BLOCKS - 1]
    picked = chosen[device_of[:, None], remote]
    slot_index = jnp.arange(1, MOST_KEY_BLOCKS)[None, :]
    tail_entries = jnp.where(slot_index < live_count[:, None], picked, jnp.arange(SEQUENCE_BLOCKS)[:, None])
    list_rows = jnp.concatenate([jnp.arange(SEQUENCE_BLOCKS)[:, None], tail_entries], axis=1).astype(jnp.int32)
    return (list_rows, live_count)


def draw_block_list(key, part):
    return plan_lists(key)[0]


def draw_block_count(key, part):
    return plan_lists(key)[1]


def block_levels(own_key, extent, shards, low, high):
    def one(position, blocks):
        draws = jax.random.uniform(jax.random.fold_in(jax.random.fold_in(own_key, 6), position), (blocks,), jnp.float32, low / len(shards), high / len(shards))
        return jnp.repeat(jnp.exp(draws), extent[position] // blocks).reshape((-1,) + (1,) * (len(extent) - position - 1))

    factor_of = one(*shards[0])
    for cut in shards[1:]:
        factor_of = factor_of * one(*cut)
    return factor_of


def gaussian(own_key, shape, scale, bound, shards=(), held_as=jnp.bfloat16):
    drawn = jax.random.normal(own_key, shape, jnp.float32) * scale
    if len(shards) > 0:
        drawn = block_levels(own_key, shape, shards, -0.22, 0.18) * drawn
    return jnp.clip(drawn, min=-bound, max=bound).astype(held_as)


def setup_inputs(seed: int = 0) -> dict:
    arg_keys = jax.random.split(jax.random.key(seed), 7)
    return {
        "input_queries": draw_input_queries(jax.random.fold_in(arg_keys[6], 71), 0),
        "input_keys": draw_input_keys(jax.random.fold_in(arg_keys[6], 71), 0),
        "input_values": gaussian(arg_keys[2], (SEQUENCE_TOKENS, KEY_VALUE_HEADS * HEAD_WIDTH), 1.0, 6.0, ((0, 128),)),
        "cotangent": gaussian(arg_keys[3], (SEQUENCE_TOKENS, QUERY_HEADS * HEAD_WIDTH), 1.0, 6.0, ((0, 128),)),
        "block_list": draw_block_list(jax.random.fold_in(arg_keys[6], 71), 0),
        "block_count": draw_block_count(jax.random.fold_in(arg_keys[6], 71), 0),
    }


NEG_FILL = -1.0e30


def round_trip(values):
    return lax.optimization_barrier(values.astype(jnp.bfloat16)).astype(jnp.float32)


def reference(input_queries, input_keys, input_values, cotangent, block_list, block_count):
    group_width = QUERY_HEADS // KEY_VALUE_HEADS
    score_scale = HEAD_WIDTH ** -0.5
    blocked_queries = input_queries.reshape(SEQUENCE_BLOCKS, BLOCK_TOKENS, KEY_VALUE_HEADS, group_width, HEAD_WIDTH)
    cotangent_blocks = cotangent.reshape(SEQUENCE_BLOCKS, BLOCK_TOKENS, KEY_VALUE_HEADS, group_width, HEAD_WIDTH)
    blocked_keys = input_keys.reshape(SEQUENCE_BLOCKS, BLOCK_TOKENS, KEY_VALUE_HEADS, HEAD_WIDTH)
    blocked_values = input_values.reshape(SEQUENCE_BLOCKS, BLOCK_TOKENS, KEY_VALUE_HEADS, HEAD_WIDTH)

    def one_block(block_tables, inputs):
        key_table, value_table = block_tables
        query_b, cot_b, table_entries, live_count = inputs
        live_keys = jnp.repeat(jnp.arange(MOST_KEY_BLOCKS) < live_count, BLOCK_TOKENS)
        selected_keys = blocked_keys[table_entries].reshape(MOST_KEY_BLOCKS * BLOCK_TOKENS, KEY_VALUE_HEADS, HEAD_WIDTH)
        selected_values = blocked_values[table_entries].reshape(MOST_KEY_BLOCKS * BLOCK_TOKENS, KEY_VALUE_HEADS, HEAD_WIDTH)

        def one_head(operands):
            query_head, cot_head, key_head, value_head = operands
            query_f = query_head.astype(jnp.float32)
            cot_f = cot_head.astype(jnp.float32)
            key_f = key_head.astype(jnp.float32)
            value_f = value_head.astype(jnp.float32)
            scores = jnp.einsum("qjd,kd->jqk", query_f, key_f) * score_scale
            scores = jnp.where(live_keys[None, None, :], scores, NEG_FILL)
            top_score = jnp.max(scores, axis=-1, keepdims=True)
            log_total = top_score + jnp.log(jnp.sum(jnp.exp(scores - top_score), axis=-1, keepdims=True))
            weights = jnp.where(live_keys[None, None, :], jnp.exp(scores - log_total), 0.0)
            weights_b = round_trip(weights)
            attended = lax.optimization_barrier(jnp.einsum("jqk,kd->qjd", weights_b, value_f).astype(jnp.bfloat16))
            row_delta = jnp.sum(attended.astype(jnp.float32) * cot_f, axis=-1)
            grad_weights = jnp.einsum("qjd,kd->jqk", cot_f, value_f)
            grad_scores = round_trip(weights * (grad_weights - row_delta.T[:, :, None]))
            grad_q = (score_scale * jnp.einsum("jqk,kd->qjd", grad_scores, key_f)).astype(jnp.bfloat16)
            key_gradient_part = score_scale * jnp.einsum("jqk,qjd->kd", grad_scores, query_f)
            value_gradient_part = jnp.einsum("jqk,qjd->kd", weights_b, cot_f)
            return attended, grad_q, key_gradient_part, value_gradient_part

        attended, grad_q, key_gradient_part, value_gradient_part = lax.map(one_head, (jnp.moveaxis(query_b, 1, 0), jnp.moveaxis(cot_b, 1, 0), jnp.moveaxis(selected_keys, 1, 0), jnp.moveaxis(selected_values, 1, 0)))
        key_gradient_part = jnp.transpose(key_gradient_part.reshape(KEY_VALUE_HEADS, MOST_KEY_BLOCKS, BLOCK_TOKENS, HEAD_WIDTH), (1, 2, 0, 3))
        value_gradient_part = jnp.transpose(value_gradient_part.reshape(KEY_VALUE_HEADS, MOST_KEY_BLOCKS, BLOCK_TOKENS, HEAD_WIDTH), (1, 2, 0, 3))
        key_table = key_table.at[table_entries].add(key_gradient_part)
        value_table = value_table.at[table_entries].add(value_gradient_part)
        return (key_table, value_table), (jnp.moveaxis(attended, 0, 1), jnp.moveaxis(grad_q, 0, 1))

    empty_table = jnp.zeros((SEQUENCE_BLOCKS, BLOCK_TOKENS, KEY_VALUE_HEADS, HEAD_WIDTH), jnp.float32)
    block_tables, outputs = lax.scan(one_block, (empty_table, empty_table), (blocked_queries, cotangent_blocks, block_list, block_count))
    attn_out = outputs[0].reshape(SEQUENCE_TOKENS, QUERY_HEADS * HEAD_WIDTH)
    grad_query = outputs[1].reshape(SEQUENCE_TOKENS, QUERY_HEADS * HEAD_WIDTH)
    key_gradient = block_tables[0].reshape(SEQUENCE_TOKENS, KEY_VALUE_HEADS * HEAD_WIDTH).astype(jnp.bfloat16)
    value_gradient = block_tables[1].reshape(SEQUENCE_TOKENS, KEY_VALUE_HEADS * HEAD_WIDTH).astype(jnp.bfloat16)
    return attn_out, grad_query, key_gradient, value_gradient
```

```python
import jax
import jax.numpy as jnp
import numpy as np
from jax import lax
from jax.experimental import pallas as pl
from jax.experimental.pallas import tpu as pltpu
from jax.sharding import PartitionSpec as P

HEAD_WIDTH=128; BLOCK_TOKENS=512; GROUP=6
SCALE=HEAD_WIDTH**-0.5
LOG2E=1.4426950408889634
NT=(((1,),(1,)),((),()))
T=BLOCK_TOKENS; D=HEAD_WIDTH

def attn_kernel(meta, q_ref, cot_ref, kv_hbm, out_ref, dq_ref, send_ref, own_ref,
                kv, pst, mst, acc, run, dqa, sems):
    f32=jnp.float32; bf=jnp.bfloat16
    def fetch(n):
        return pltpu.make_async_copy(kv_hbm.at[meta[n]], kv.at[n], sems.at[n])
    for n in range(16):
        @pl.when(n % 8 < meta[48 + n//8])
        def _(): fetch(n).start()
    for b in range(2):
        rows=slice(b*T,(b+1)*T)
        cnt=meta[48+b]
        acc[...]=jnp.zeros_like(acc)
        run[0]=jnp.full((8,T),-1e30,f32)
        run[1]=jnp.zeros((8,T),f32)
        def fwd(i, _):
            fetch(b*8+i).wait()
            k=kv[b*8+i,:,:D]; vt=kv[b*8+i,:,D:].T
            for j in range(GROUP):
                qj=q_ref[rows,j*D:(j+1)*D]
                s=lax.dot_general(k,qj,NT,preferred_element_type=f32)
                mx=jnp.max(s,axis=0,keepdims=True)*(SCALE*LOG2E)
                p=jnp.exp2(s*(SCALE*LOG2E)-mx)
                li=jnp.sum(p,axis=0,keepdims=True)
                pb=p.astype(bf)
                pst[i,:,j*T:(j+1)*T]=pb
                ot=jnp.dot(vt,pb,preferred_element_type=f32)
                mo=run[0,j:j+1]; mn=jnp.maximum(mo,mx)
                al=jnp.exp2(mo-mn); be=jnp.exp2(mx-mn)
                mst[i,j:j+1]=mx
                run[0,j:j+1]=mn
                run[1,j:j+1]=run[1,j:j+1]*al+li*be
                acc[j]=acc[j]*al+ot*be
            return 0
        lax.fori_loop(0,cnt,fwd,0)
        for j in range(GROUP):
            o=(acc[j]/run[1,j:j+1]).astype(bf)
            out_ref[rows,j*D:(j+1)*D]=o.T
            ct=cot_ref[rows,j*D:(j+1)*D].T
            run[2,j:j+1]=jnp.sum(o.astype(f32)*ct.astype(f32),axis=0,keepdims=True)
        dqa[...]=jnp.zeros_like(dqa)
        def bwd(i,_):
            k=kv[b*8+i,:,:D]; v=kv[b*8+i,:,D:]; kt=k.T
            dk=jnp.zeros((T,D),f32); dv=jnp.zeros((T,D),f32)
            for j in range(GROUP):
                qj=q_ref[rows,j*D:(j+1)*D]; cj=cot_ref[rows,j*D:(j+1)*D]
                dp=lax.dot_general(v,cj,NT,preferred_element_type=f32)
                r=jnp.exp2(mst[i,j:j+1]-run[0,j:j+1])/run[1,j:j+1]
                pn=pst[i,:,j*T:(j+1)*T].astype(f32)*r
                ds=(pn*(dp-run[2,j:j+1])).astype(bf)
                dqa[j]+=jnp.dot(kt,ds,preferred_element_type=f32)
                dk+=jnp.dot(ds,qj,preferred_element_type=f32)
                dv+=jnp.dot(pn.astype(bf),cj,preferred_element_type=f32)
            dk=dk*SCALE
            d=meta[32+b*8+i]; sh=meta[16+b*8+i]
            @pl.when(i==0)
            def _():
                own_ref[b,:,:D]=dk; own_ref[b,:,D:]=dv
            @pl.when(jnp.logical_and(i>0, sh==0))
            def _():
                send_ref[d,:,:D]=dk.astype(bf); send_ref[d,:,D:]=dv.astype(bf)
            @pl.when(jnp.logical_and(i>0, sh!=0))
            def _():
                send_ref[d,:,:D]=(send_ref[d,:,:D].astype(f32)+dk).astype(bf)
                send_ref[d,:,D:]=(send_ref[d,:,D:].astype(f32)+dv).astype(bf)
            return 0
        lax.fori_loop(0,cnt,bwd,0)
        for j in range(GROUP):
            dq_ref[rows,j*D:(j+1)*D]=(dqa[j]*SCALE).astype(bf).T

def attn(meta,q,cot,kvt):
    f32=jnp.float32; bf=jnp.bfloat16
    V=pl.BlockSpec(memory_space=pltpu.VMEM)
    return pl.pallas_call(attn_kernel,
        out_shape=(jax.ShapeDtypeStruct((2*T,GROUP*D),bf),)*2+(jax.ShapeDtypeStruct((16,T,2*D),bf),jax.ShapeDtypeStruct((2,T,2*D),f32)),
        in_specs=[pl.BlockSpec(memory_space=pltpu.SMEM),V,V,pl.BlockSpec(memory_space=pl.ANY)],
        out_specs=(V,)*4,
        scratch_shapes=[pltpu.VMEM((16,T,2*D),bf),pltpu.VMEM((8,T,GROUP*T),bf),pltpu.VMEM((8,8,T),f32),
            pltpu.VMEM((GROUP,D,T),f32),pltpu.VMEM((3,8,T),f32),pltpu.VMEM((GROUP,D,T),f32),pltpu.SemaphoreType.DMA((16,))],
        compiler_params=pltpu.CompilerParams(vmem_limit_bytes=62*1024*1024),
        )(meta,q,cot,kvt)


def plan(block_list, ctx):
    rows = lax.dynamic_slice_in_dim(block_list, 2 * ctx, 2, 0)
    owner = rows // 2
    shared = jnp.any(owner[1][:, None] == owner[0][None, :], axis=1).astype(jnp.int32)
    return rows, owner, shared


def heads_in(x):
    width = x.shape[1] // 8
    x = jnp.transpose(x.reshape(x.shape[0], 8, width), (1, 0, 2))
    return lax.all_to_all(x, "head", split_axis=0, concat_axis=0, tiled=True).reshape(-1, width)


def heads_out(x):
    width = x.shape[1]
    x = lax.all_to_all(x.reshape(8, -1, width), "head", split_axis=0, concat_axis=0, tiled=True)
    return jnp.transpose(x, (1, 0, 2)).reshape(-1, 8 * width)


def shards(input_queries, input_keys, input_values, cotangent, block_list, block_count):
    ctx = lax.axis_index("ctx")
    keys, values = heads_in(input_keys), heads_in(input_values)
    own_table = jnp.concatenate([keys, values], axis=1).reshape(2, T, 2 * D)
    table = lax.all_gather(own_table, "ctx", axis=0, tiled=True)
    queries, cot = heads_in(input_queries), heads_in(cotangent)
    rows, owner, shared = plan(block_list, ctx)
    counts = lax.dynamic_slice_in_dim(block_count, 2 * ctx, 2, 0)
    meta = jnp.concatenate(
        [rows.reshape(16), jnp.zeros(8, jnp.int32), shared, owner.reshape(16), counts, jnp.zeros(14, jnp.int32)]
    )
    out, dq, send, own = attn(meta, queries, cot, table)
    got = lax.all_to_all(send, "ctx", split_axis=0, concat_axis=0, tiled=True)
    mine = 2 * ctx + jnp.arange(2)
    named = jnp.any(block_list.reshape(16, 16)[:, :, None] == mine[None, None, :], axis=1)
    named = jnp.logical_and(named, (jnp.arange(16) != ctx)[:, None])
    parts = jnp.where(named[:, :, None, None], got[:, None], jnp.zeros((), jnp.bfloat16))
    grads = (own + jnp.sum(parts.astype(jnp.float32), axis=0)).astype(jnp.bfloat16).reshape(2 * T, 2 * D)
    return heads_out(out), heads_out(dq), heads_out(grads[:, :D]), heads_out(grads[:, D:])


def solution(mesh):
    spec = P(("ctx", "head"), None)
    return jax.shard_map(
        shards,
        mesh=mesh,
        in_specs=(spec,) * 4 + (P(), P()),
        out_specs=(spec,) * 4,
        check_vma=False,
    )
```

```python
import jax
import jax.numpy as jnp
from jax import lax
from jax.experimental import pallas as pl
from jax.experimental.pallas import tpu as pltpu
from jax.sharding import PartitionSpec as P

HEAD_WIDTH=128; BLOCK_TOKENS=512; GROUP=6
SCALE=HEAD_WIDTH**-0.5
LOG2E=1.4426950408889634
NT=(((1,),(1,)),((),()))
T=BLOCK_TOKENS; D=HEAD_WIDTH

def attn_kernel(meta, q_ref, cot_ref, kv_hbm, out_ref, dq_ref, send_ref, own_ref,
                kv, pst, mst, acc, run, dqa, sems):
    f32=jnp.float32; bf=jnp.bfloat16
    def fetch(n):
        return pltpu.make_async_copy(kv_hbm.at[meta[n]], kv.at[n], sems.at[n])
    for n in range(16):
        @pl.when(n % 8 < meta[48 + n//8])
        def _(): fetch(n).start()
    for b in range(2):
        rows=slice(b*T,(b+1)*T)
        cnt=meta[48+b]
        acc[...]=jnp.zeros_like(acc)
        run[0]=jnp.full((8,T),-1e30,f32)
        run[1]=jnp.zeros((8,T),f32)
        def fwd(i, _):
            fetch(b*8+i).wait()
            k=kv[b*8+i,:,:D]; vt=kv[b*8+i,:,D:].T
            for j in range(GROUP):
                qj=q_ref[rows,j*D:(j+1)*D]
                s=lax.dot_general(k,qj,NT,preferred_element_type=f32)
                mx=jnp.max(s,axis=0,keepdims=True)*(SCALE*LOG2E)
                p=jnp.exp2(s*(SCALE*LOG2E)-mx)
                li=jnp.sum(p,axis=0,keepdims=True)
                pb=p.astype(bf)
                pst[i,:,j*T:(j+1)*T]=pb
                ot=jnp.dot(vt,pb,preferred_element_type=f32)
                mo=run[0,j:j+1]; mn=jnp.maximum(mo,mx)
                al=jnp.exp2(mo-mn); be=jnp.exp2(mx-mn)
                mst[i,j:j+1]=mx
                run[0,j:j+1]=mn
                run[1,j:j+1]=run[1,j:j+1]*al+li*be
                acc[j]=acc[j]*al+ot*be
            return 0
        lax.fori_loop(0,cnt,fwd,0)
        for j in range(GROUP):
            o=(acc[j]/run[1,j:j+1]).astype(bf)
            out_ref[rows,j*D:(j+1)*D]=o.T
            ct=cot_ref[rows,j*D:(j+1)*D].T
            run[2,j:j+1]=jnp.sum(o.astype(f32)*ct.astype(f32),axis=0,keepdims=True)
        dqa[...]=jnp.zeros_like(dqa)
        def bwd(i,_):
            k=kv[b*8+i,:,:D]; v=kv[b*8+i,:,D:]; kt=k.T
            dk=jnp.zeros((T,D),f32); dv=jnp.zeros((T,D),f32)
            for j in range(GROUP):
                qj=q_ref[rows,j*D:(j+1)*D]; cj=cot_ref[rows,j*D:(j+1)*D]
                dp=lax.dot_general(v,cj,NT,preferred_element_type=f32)
                r=jnp.exp2(mst[i,j:j+1]-run[0,j:j+1])/run[1,j:j+1]
                pn=pst[i,:,j*T:(j+1)*T].astype(f32)*r
                ds=(pn*(dp-run[2,j:j+1])).astype(bf)
                dqa[j]+=jnp.dot(kt,ds,preferred_element_type=f32)
                dk+=jnp.dot(ds,qj,preferred_element_type=f32)
                dv+=jnp.dot(pn.astype(bf),cj,preferred_element_type=f32)
            dk=dk*SCALE
            d=meta[32+b*8+i]; sh=meta[16+b*8+i]
            @pl.when(i==0)
            def _():
                own_ref[b,:,:D]=dk; own_ref[b,:,D:]=dv
            @pl.when(jnp.logical_and(i>0, sh==0))
            def _():
                send_ref[d,:,:D]=dk.astype(bf); send_ref[d,:,D:]=dv.astype(bf)
            @pl.when(jnp.logical_and(i>0, sh!=0))
            def _():
                send_ref[d,:,:D]=(send_ref[d,:,:D].astype(f32)+dk).astype(bf)
                send_ref[d,:,D:]=(send_ref[d,:,D:].astype(f32)+dv).astype(bf)
            return 0
        lax.fori_loop(0,cnt,bwd,0)
        for j in range(GROUP):
            dq_ref[rows,j*D:(j+1)*D]=(dqa[j]*SCALE).astype(bf).T

def attn(meta,q,cot,kvt):
    f32=jnp.float32; bf=jnp.bfloat16
    V=pl.BlockSpec(memory_space=pltpu.VMEM)
    return pl.pallas_call(attn_kernel,
        out_shape=(jax.ShapeDtypeStruct((2*T,GROUP*D),bf),)*2+(jax.ShapeDtypeStruct((16,T,2*D),bf),jax.ShapeDtypeStruct((2,T,2*D),f32)),
        in_specs=[pl.BlockSpec(memory_space=pltpu.SMEM),V,V,pl.BlockSpec(memory_space=pl.ANY)],
        out_specs=(V,)*4,
        scratch_shapes=[pltpu.VMEM((16,T,2*D),bf),pltpu.VMEM((8,T,GROUP*T),bf),pltpu.VMEM((8,8,T),f32),
            pltpu.VMEM((GROUP,D,T),f32),pltpu.VMEM((3,8,T),f32),pltpu.VMEM((GROUP,D,T),f32),pltpu.SemaphoreType.DMA((16,))],
        compiler_params=pltpu.CompilerParams(vmem_limit_bytes=62*1024*1024),
        )(meta,q,cot,kvt)


CTX = 16
HEADS = 8
MESH = pl.DeviceIdType.MESH
QW = GROUP * D


def greet(ctx, head):
    barrier = pltpu.get_barrier_semaphore()

    def ctx_peer(n, _):
        pl.semaphore_signal(barrier, inc=1, device_id=(lax.rem(ctx + n, CTX), head), device_id_type=MESH)
        return 0

    def head_peer(n, _):
        pl.semaphore_signal(barrier, inc=1, device_id=(ctx, lax.rem(head + n, HEADS)), device_id_type=MESH)
        return 0

    lax.fori_loop(1, CTX, ctx_peer, 0)
    lax.fori_loop(1, HEADS, head_peer, 0)
    pl.semaphore_wait(barrier, CTX + HEADS - 2)


def cols(index, width):
    return pl.ds(pl.multiple_of(index * width, width), width)


def spread_kernel(pick, q_ref, k_ref, v_ref, c_ref, qh_ref, ch_ref, table_ref,
                  kv_own, stage, head_send, head_recv, ctx_send, ctx_recv, local_sem):
    ctx, head = lax.axis_index("ctx"), lax.axis_index("head")
    greet(ctx, head)
    tokens = k_ref.shape[0]
    arrays = (
        (k_ref, lambda s: kv_own.at[cols(s, tokens), :D], D),
        (v_ref, lambda s: kv_own.at[cols(s, tokens), D:], D),
        (q_ref, lambda s: qh_ref.at[cols(s, tokens)], QW),
        (c_ref, lambda s: ch_ref.at[cols(s, tokens)], QW),
    )

    def send(a, to, frm):
        ref, place, width = arrays[a]
        return pltpu.make_async_remote_copy(
            ref.at[:, cols(to, width)], place(frm), head_send.at[a, to], head_recv.at[a, frm],
            device_id=(ctx, to), device_id_type=MESH)

    def keep(a):
        ref, place, width = arrays[a]
        return pltpu.make_async_copy(ref.at[:, cols(head, width)], place(head), local_sem.at[a])

    def start_kv(n, _):
        to = lax.rem(head + n, HEADS)
        send(0, to, head).start()
        send(1, to, head).start()
        return 0

    def start_q(n, _):
        to = lax.rem(head + n, HEADS)
        send(2, to, head).start()
        send(3, to, head).start()
        return 0

    for a in range(4):
        keep(a).start()
    lax.fori_loop(1, HEADS, start_kv, 0)
    lax.fori_loop(1, HEADS, start_q, 0)

    def take_kv(n, _):
        frm = lax.rem(head + n, HEADS)
        send(0, frm, frm).wait_recv()
        send(1, frm, frm).wait_recv()
        return 0

    keep(0).wait()
    keep(1).wait()
    lax.fori_loop(1, HEADS, take_kv, 0)

    own = [pltpu.make_async_copy(kv_own.at[b * T:(b + 1) * T], table_ref.at[CTX + b], local_sem.at[4 + b])
           for b in range(2)]
    for copy in own:
        copy.start()

    def push(to, frm):
        return pltpu.make_async_remote_copy(
            stage.at[to], table_ref.at[frm], ctx_send.at[to], ctx_recv.at[frm],
            device_id=(to, head), device_id_type=MESH)

    def start_push(n, _):
        to = lax.rem(ctx + n, CTX)
        stage[to] = jnp.where(pick[to] == 1, kv_own[T:], kv_own[:T])
        push(to, ctx).start()
        return 0

    lax.fori_loop(1, CTX, start_push, 0)

    def end_push(n, _):
        peer = lax.rem(ctx + n, CTX)
        push(peer, ctx).wait_send()
        push(peer, peer).wait_recv()
        return 0

    def end_head(n, _):
        peer = lax.rem(head + n, HEADS)
        for a in range(4):
            send(a, peer, head).wait_send()
        for a in (2, 3):
            send(a, peer, peer).wait_recv()
        return 0

    lax.fori_loop(1, HEADS, end_head, 0)
    keep(2).wait()
    keep(3).wait()
    for copy in own:
        copy.wait()
    lax.fori_loop(1, CTX, end_push, 0)


def spread(pick, q, k, v, cot):
    bf = jnp.bfloat16
    any_spec = pl.BlockSpec(memory_space=pl.ANY)
    return pl.pallas_call(
        spread_kernel,
        out_shape=(jax.ShapeDtypeStruct((2 * T, QW), bf), jax.ShapeDtypeStruct((2 * T, QW), bf),
                   jax.ShapeDtypeStruct((CTX + 2, T, 2 * D), bf)),
        in_specs=[pl.BlockSpec(memory_space=pltpu.SMEM)] + [any_spec] * 4,
        out_specs=(any_spec,) * 3,
        scratch_shapes=[
            pltpu.VMEM((2 * T, 2 * D), bf),
            pltpu.VMEM((CTX, T, 2 * D), bf),
            pltpu.SemaphoreType.DMA((4, HEADS)),
            pltpu.SemaphoreType.DMA((4, HEADS)),
            pltpu.SemaphoreType.DMA((CTX,)),
            pltpu.SemaphoreType.DMA((CTX,)),
            pltpu.SemaphoreType.DMA((6,)),
        ],
        compiler_params=pltpu.CompilerParams(collective_id=0, has_side_effects=True, vmem_limit_bytes=60 * 2**20),
    )(pick, q, k, v, cot)


def collect_kernel(code, out_ref, dq_ref, send_ref, own_ref, o_res, dq_res, dk_res, dv_res,
                   got, total, grads, ctx_send, ctx_recv, head_send, head_recv, local_sem):
    f32, bf = jnp.float32, jnp.bfloat16
    ctx, head = lax.axis_index("ctx"), lax.axis_index("head")
    greet(ctx, head)
    tokens = o_res.shape[0]
    arrays = (
        (lambda to: out_ref.at[cols(to, tokens)], lambda s: o_res.at[:, cols(s, QW)]),
        (lambda to: dq_ref.at[cols(to, tokens)], lambda s: dq_res.at[:, cols(s, QW)]),
        (lambda to: grads.at[cols(to, tokens), :D], lambda s: dk_res.at[:, cols(s, D)]),
        (lambda to: grads.at[cols(to, tokens), D:], lambda s: dv_res.at[:, cols(s, D)]),
    )

    def push(to, frm):
        return pltpu.make_async_remote_copy(
            send_ref.at[to], got.at[frm], ctx_send.at[to], ctx_recv.at[frm],
            device_id=(to, head), device_id_type=MESH)

    def send(a, to, frm):
        source, place = arrays[a]
        return pltpu.make_async_remote_copy(
            source(to), place(frm), head_send.at[a, to], head_recv.at[a, frm],
            device_id=(ctx, to), device_id_type=MESH)

    def keep(a):
        source, place = arrays[a]
        return pltpu.make_async_copy(source(head), place(head), local_sem.at[a])

    def start_push(n, _):
        push(lax.rem(ctx + n, CTX), ctx).start()
        return 0

    def start_out(n, _):
        to = lax.rem(head + n, HEADS)
        send(0, to, head).start()
        send(1, to, head).start()
        return 0

    first = pltpu.make_async_copy(own_ref, total, local_sem.at[4])
    first.start()
    lax.fori_loop(1, CTX, start_push, 0)
    lax.fori_loop(1, HEADS, start_out, 0)
    keep(0).start()
    keep(1).start()
    first.wait()

    def add(n, _):
        frm = lax.rem(ctx + n, CTX)
        push(frm, frm).wait_recv()
        mark = code[frm]
        part = got[frm].astype(f32)
        total[0] += jnp.where(mark == 1, part, 0.0)
        total[1] += jnp.where(mark == 2, part, 0.0)
        return 0

    lax.fori_loop(1, CTX, add, 0)
    for b in range(2):
        grads[b * T:(b + 1) * T] = total[b].astype(bf)

    def start_grads(n, _):
        to = lax.rem(head + n, HEADS)
        send(2, to, head).start()
        send(3, to, head).start()
        return 0

    lax.fori_loop(1, HEADS, start_grads, 0)
    keep(2).start()
    keep(3).start()

    def end_push(n, _):
        push(lax.rem(ctx + n, CTX), ctx).wait_send()
        return 0

    def end_head(n, _):
        peer = lax.rem(head + n, HEADS)
        for a in range(4):
            send(a, peer, head).wait_send()
            send(a, peer, peer).wait_recv()
        return 0

    lax.fori_loop(1, CTX, end_push, 0)
    lax.fori_loop(1, HEADS, end_head, 0)
    for a in range(4):
        keep(a).wait()


def collect(code, out, dq, send, own):
    f32, bf = jnp.float32, jnp.bfloat16
    any_spec = pl.BlockSpec(memory_space=pl.ANY)
    tokens = 2 * T // HEADS
    wide = jax.ShapeDtypeStruct((tokens, HEADS * QW), bf)
    thin = jax.ShapeDtypeStruct((tokens, HEADS * D), bf)
    return pl.pallas_call(
        collect_kernel,
        out_shape=(wide, wide, thin, thin),
        in_specs=[pl.BlockSpec(memory_space=pltpu.SMEM)] + [any_spec] * 4,
        out_specs=(any_spec,) * 4,
        scratch_shapes=[
            pltpu.VMEM((CTX, T, 2 * D), bf),
            pltpu.VMEM((2, T, 2 * D), f32),
            pltpu.VMEM((2 * T, 2 * D), bf),
            pltpu.SemaphoreType.DMA((CTX,)),
            pltpu.SemaphoreType.DMA((CTX,)),
            pltpu.SemaphoreType.DMA((4, HEADS)),
            pltpu.SemaphoreType.DMA((4, HEADS)),
            pltpu.SemaphoreType.DMA((5,)),
        ],
        compiler_params=pltpu.CompilerParams(collective_id=1, has_side_effects=True, vmem_limit_bytes=60 * 2**20),
    )(code, out, dq, send, own)


def shards(input_queries, input_keys, input_values, cotangent, block_list, block_count):
    ctx = lax.axis_index("ctx")
    rows = lax.dynamic_slice_in_dim(block_list, 2 * ctx, 2, 0)
    owner = rows // 2
    slots = jnp.where(jnp.arange(8)[None, :] == 0, CTX + jnp.arange(2)[:, None], owner)
    shared = jnp.any(owner[1][:, None] == owner[0][None, :], axis=1).astype(jnp.int32)
    counts = lax.dynamic_slice_in_dim(block_count, 2 * ctx, 2, 0)
    meta = jnp.concatenate(
        [slots.reshape(16), jnp.zeros(8, jnp.int32), shared, owner.reshape(16), counts, jnp.zeros(14, jnp.int32)]
    ).astype(jnp.int32)
    lists = block_list.reshape(CTX, 16)
    named = [jnp.any(lists == 2 * ctx + b, axis=1) for b in range(2)]
    pick = named[1].astype(jnp.int32)
    code = named[0].astype(jnp.int32) + 2 * pick
    queries, cot, table = spread(pick, input_queries, input_keys, input_values, cotangent)
    out, dq, send, own = attn(meta, queries, cot, table)
    return collect(code, out, dq, send, own)


def solution(mesh):
    spec = P(("ctx", "head"), None)
    return jax.shard_map(
        shards,
        mesh=mesh,
        in_specs=(spec,) * 4 + (P(), P()),
        out_specs=(spec,) * 4,
        check_vma=False,
    )
```

```python
import jax
import jax.numpy as jnp
from jax import lax
from jax.experimental import pallas as pl
from jax.experimental.pallas import tpu as pltpu
from jax.sharding import PartitionSpec as P

D = 128
T = 512
GROUP = 6
QW = GROUP * D
SIDE = 4
CTX = SIDE * SIDE
HEADS = 8
MOST = 8
SCALE = D**-0.5
LOG2E = 1.4426950408889634
NT = (((1,), (1,)), ((), ()))
MESH = pl.DeviceIdType.MESH


def attn_kernel(lists, counts, q_ref, cot_ref, kv_hbm, out_ref, dq_ref, send_ref, own_ref,
                kv, pst, mst, acc, run, dqa, sems):
    ctx = lax.axis_index("ctx")

    def owner(b, i):
        return lists[2 * ctx + b, i] // 2

    f32=jnp.float32; bf=jnp.bfloat16
    def fetch(b, i):
        slot = jnp.where(i == 0, CTX + b, owner(b, i))
        return pltpu.make_async_copy(kv_hbm.at[slot], kv.at[b * MOST + i], sems.at[b * MOST + i])

    def prefetch(b):
        def one(i, _):
            fetch(b, i).start()
            return 0
        lax.fori_loop(0, counts[2 * ctx + b], one, 0)

    prefetch(0)
    prefetch(1)
    for b in range(2):
        rows=slice(b*T,(b+1)*T)
        cnt=counts[2*ctx+b]
        acc[...]=jnp.zeros_like(acc)
        run[0]=jnp.full((8,T),-1e30,f32)
        run[1]=jnp.zeros((8,T),f32)
        def fwd(i, _):
            fetch(b, i).wait()
            k=kv[b*8+i,:,:D]; vt=kv[b*8+i,:,D:].T
            for j in range(GROUP):
                qj=q_ref[rows,j*D:(j+1)*D]
                s=lax.dot_general(k,qj,NT,preferred_element_type=f32)
                mx=jnp.max(s,axis=0,keepdims=True)*(SCALE*LOG2E)
                p=jnp.exp2(s*(SCALE*LOG2E)-mx)
                li=jnp.sum(p,axis=0,keepdims=True)
                pb=p.astype(bf)
                pst[i,:,j*T:(j+1)*T]=pb
                ot=jnp.dot(vt,pb,preferred_element_type=f32)
                mo=run[0,j:j+1]; mn=jnp.maximum(mo,mx)
                al=jnp.exp2(mo-mn); be=jnp.exp2(mx-mn)
                mst[i,j:j+1]=mx
                run[0,j:j+1]=mn
                run[1,j:j+1]=run[1,j:j+1]*al+li*be
                acc[j]=acc[j]*al+ot*be
            return 0
        lax.fori_loop(0,cnt,fwd,0)
        for j in range(GROUP):
            o=(acc[j]/run[1,j:j+1]).astype(bf)
            out_ref[rows,j*D:(j+1)*D]=o.T
            ct=cot_ref[rows,j*D:(j+1)*D].T
            run[2,j:j+1]=jnp.sum(o.astype(f32)*ct.astype(f32),axis=0,keepdims=True)
        dqa[...]=jnp.zeros_like(dqa)
        def bwd(i,_):
            k=kv[b*8+i,:,:D]; v=kv[b*8+i,:,D:]; kt=k.T
            dk=jnp.zeros((T,D),f32); dv=jnp.zeros((T,D),f32)
            for j in range(GROUP):
                qj=q_ref[rows,j*D:(j+1)*D]; cj=cot_ref[rows,j*D:(j+1)*D]
                dp=lax.dot_general(v,cj,NT,preferred_element_type=f32)
                r=jnp.exp2(mst[i,j:j+1]-run[0,j:j+1])/run[1,j:j+1]
                pn=pst[i,:,j*T:(j+1)*T].astype(f32)*r
                ds=(pn*(dp-run[2,j:j+1])).astype(bf)
                dqa[j]+=jnp.dot(kt,ds,preferred_element_type=f32)
                dk+=jnp.dot(ds,qj,preferred_element_type=f32)
                dv+=jnp.dot(pn.astype(bf),cj,preferred_element_type=f32)
            dk=dk*SCALE
            d=owner(b, i)
            sh=jnp.int32(0)
            if b == 1:
                for n in range(1, MOST):
                    sh += (owner(0, n) == d).astype(jnp.int32)
            @pl.when(i==0)
            def _():
                own_ref[0,b]=dk; own_ref[1,b]=dv
            @pl.when(jnp.logical_and(i>0, sh==0))
            def _():
                send_ref[d,:,:D]=dk.astype(bf); send_ref[d,:,D:]=dv.astype(bf)
            @pl.when(jnp.logical_and(i>0, sh!=0))
            def _():
                send_ref[d,:,:D]=(send_ref[d,:,:D].astype(f32)+dk).astype(bf)
                send_ref[d,:,D:]=(send_ref[d,:,D:].astype(f32)+dv).astype(bf)
            return 0
        lax.fori_loop(0,cnt,bwd,0)
        for j in range(GROUP):
            dq_ref[rows,j*D:(j+1)*D]=(dqa[j]*SCALE).astype(bf).T

def attn(lists,counts,q,cot,kvt):
    f32=jnp.float32; bf=jnp.bfloat16
    V=pl.BlockSpec(memory_space=pltpu.VMEM)
    return pl.pallas_call(attn_kernel,
        out_shape=(jax.ShapeDtypeStruct((2*T,GROUP*D),bf),)*2+(jax.ShapeDtypeStruct((16,T,2*D),bf),jax.ShapeDtypeStruct((2,2,T,D),f32)),
        in_specs=[pl.BlockSpec(memory_space=pltpu.SMEM)]*2+[V,V,pl.BlockSpec(memory_space=pl.ANY)],
        out_specs=(V,)*4,
        scratch_shapes=[pltpu.VMEM((16,T,2*D),bf),pltpu.VMEM((8,T,GROUP*T),bf),pltpu.VMEM((8,8,T),f32),
            pltpu.VMEM((GROUP,D,T),f32),pltpu.VMEM((3,8,T),f32),pltpu.VMEM((GROUP,D,T),f32),pltpu.SemaphoreType.DMA((16,))],
        compiler_params=pltpu.CompilerParams(vmem_limit_bytes=62*1024*1024),
        )(lists,counts,q,cot,kvt)


def greet(ctx, head):
    barrier = pltpu.get_barrier_semaphore()
    y, x = ctx // SIDE, lax.rem(ctx, SIDE)

    def line(n, _):
        pl.semaphore_signal(barrier, inc=1, device_id=(y * SIDE + lax.rem(x + n, SIDE), head), device_id_type=MESH)
        pl.semaphore_signal(barrier, inc=1, device_id=(lax.rem(y + n, SIDE) * SIDE + x, head), device_id_type=MESH)
        return 0

    def head_peer(n, _):
        pl.semaphore_signal(barrier, inc=1, device_id=(ctx, lax.rem(head + n, HEADS)), device_id_type=MESH)
        return 0

    lax.fori_loop(1, SIDE, line, 0)
    lax.fori_loop(1, HEADS, head_peer, 0)
    pl.semaphore_wait(barrier, 2 * (SIDE - 1) + HEADS - 1)


def cols(index, width):
    return pl.ds(pl.multiple_of(index * width, width), width)


def lists_block(lists, ctx, block):
    hits = jnp.int32(0)
    for b in range(2):
        for i in range(1, MOST):
            hits += (lists[2 * ctx + b, i] == block).astype(jnp.int32)
    return hits > 0


def spread_kernel(lists, q_ref, k_ref, v_ref, c_ref, qh_ref, ch_ref, table_ref,
                  lines, stage, head_send, head_recv, line_send, line_recv, push_send, push_recv, local_sem, fill_sem):
    ctx, head = lax.axis_index("ctx"), lax.axis_index("head")
    y, x = ctx // SIDE, lax.rem(ctx, SIDE)
    here = (x, y)
    greet(ctx, head)
    tokens = k_ref.shape[0]
    arrays = (
        (k_ref, lambda s: lines.at[0, x, cols(s, tokens)], D),
        (v_ref, lambda s: lines.at[1, y, cols(s, tokens)], D),
        (q_ref, lambda s: qh_ref.at[cols(s, tokens)], QW),
        (c_ref, lambda s: ch_ref.at[cols(s, tokens)], QW),
    )

    def at(kind, along, across):
        return across * SIDE + along if kind == 0 else along * SIDE + across

    def send(a, to, frm):
        ref, place, width = arrays[a]
        return pltpu.make_async_remote_copy(
            ref.at[:, cols(to, width)], place(frm), head_send.at[a, to], head_recv.at[a, frm],
            device_id=(ctx, to), device_id_type=MESH)

    def keep(a):
        ref, place, width = arrays[a]
        return pltpu.make_async_copy(ref.at[:, cols(head, width)], place(head), local_sem.at[a])

    def each_head(arrays_used, act):
        def one(n, _):
            peer = lax.rem(head + n, HEADS)
            for a in arrays_used:
                act(a, peer)
            return 0
        lax.fori_loop(1, HEADS, one, 0)

    for a in range(4):
        keep(a).start()
    each_head((0, 1), lambda a, p: send(a, p, head).start())
    each_head((2, 3), lambda a, p: send(a, p, head).start())
    keep(0).wait()
    keep(1).wait()
    each_head((0, 1), lambda a, p: send(a, p, p).wait_recv())

    def share(kind, to, frm):
        return pltpu.make_async_remote_copy(
            lines.at[kind, frm], lines.at[kind, frm], line_send.at[kind, to], line_recv.at[kind, frm],
            device_id=(at(kind, to, here[1 - kind]), head), device_id_type=MESH)

    def push(kind, to, along, frm):
        source = at(kind, along, frm)
        return pltpu.make_async_remote_copy(
            stage.at[kind, to, along], table_ref.at[source, :, kind * D:(kind + 1) * D],
            push_send.at[kind, to, along], push_recv.at[kind, frm, along],
            device_id=(at(kind, here[kind], to), head), device_id_type=MESH)

    def fill(kind, along):
        mine = here[1 - kind]
        return pltpu.make_async_copy(
            stage.at[kind, mine, along], table_ref.at[at(kind, along, mine), :, kind * D:(kind + 1) * D],
            fill_sem.at[kind, along])

    def own(kind, b):
        return pltpu.make_async_copy(
            lines.at[kind, here[kind], b * T:(b + 1) * T], table_ref.at[CTX + b, :, kind * D:(kind + 1) * D],
            local_sem.at[4 + 2 * kind + b])

    def prepare(kind, to, along):
        source = at(kind, along, here[1 - kind])
        second = lists_block(lists, at(kind, here[kind], to), 2 * source + 1)
        stage[kind, to, along] = jnp.where(second, lines[kind, along, T:], lines[kind, along, :T])

    for n in (1, 3, 2):
        for kind in range(2):
            share(kind, lax.rem(here[kind] + n, SIDE), here[kind]).start()
    for kind in range(2):
        for b in range(2):
            own(kind, b).start()

    def push_all(m, _):
        for kind in range(2):
            along = lax.rem(here[kind] + m, SIDE)

            @pl.when(m > 0)
            def _():
                share(kind, along, along).wait_recv()

            for n in range(1, SIDE):
                to = lax.rem(here[1 - kind] + n, SIDE)
                prepare(kind, to, along)
                push(kind, to, along, here[1 - kind]).start()

            @pl.when(m > 0)
            def _():
                prepare(kind, here[1 - kind], along)
                fill(kind, along).start()
        return 0

    lax.fori_loop(0, SIDE, push_all, 0)

    each_head(range(4), lambda a, p: send(a, p, head).wait_send())
    each_head((2, 3), lambda a, p: send(a, p, p).wait_recv())
    keep(2).wait()
    keep(3).wait()

    def drain(m, _):
        for kind in range(2):
            along = lax.rem(here[kind] + m, SIDE)

            @pl.when(m > 0)
            def _():
                share(kind, along, here[kind]).wait_send()
                fill(kind, along).wait()

            for n in range(1, SIDE):
                peer = lax.rem(here[1 - kind] + n, SIDE)
                push(kind, peer, along, here[1 - kind]).wait_send()
                push(kind, peer, along, peer).wait_recv()
        return 0

    lax.fori_loop(0, SIDE, drain, 0)
    for kind in range(2):
        for b in range(2):
            own(kind, b).wait()


def spread(lists, q, k, v, cot):
    bf = jnp.bfloat16
    any_spec = pl.BlockSpec(memory_space=pl.ANY)
    dma = pltpu.SemaphoreType.DMA
    return pl.pallas_call(
        spread_kernel,
        out_shape=(jax.ShapeDtypeStruct((2 * T, QW), bf), jax.ShapeDtypeStruct((2 * T, QW), bf),
                   jax.ShapeDtypeStruct((CTX + 2, T, 2 * D), bf)),
        in_specs=[pl.BlockSpec(memory_space=pltpu.SMEM)] + [any_spec] * 4,
        out_specs=(any_spec,) * 3,
        scratch_shapes=[
            pltpu.VMEM((2, SIDE, 2 * T, D), bf),
            pltpu.VMEM((2, SIDE, SIDE, T, D), bf),
            dma((4, HEADS)), dma((4, HEADS)), dma((2, SIDE)), dma((2, SIDE)),
            dma((2, SIDE, SIDE)), dma((2, SIDE, SIDE)), dma((8,)), dma((2, SIDE)),
        ],
        compiler_params=pltpu.CompilerParams(collective_id=0, has_side_effects=True, vmem_limit_bytes=60 * 2**20),
    )(lists, q, k, v, cot)


def collect_kernel(lists, out_ref, dq_ref, send_ref, own_ref, o_res, dq_res, dk_res, dv_res,
                   first, sums, second, total, grads,
                   head_send, head_recv, line_send, line_recv, push_send, push_recv, local_sem):
    f32, bf = jnp.float32, jnp.bfloat16
    ctx, head = lax.axis_index("ctx"), lax.axis_index("head")
    y, x = ctx // SIDE, lax.rem(ctx, SIDE)
    here = (x, y)
    greet(ctx, head)
    tokens = o_res.shape[0]
    arrays = (
        (lambda to: out_ref.at[cols(to, tokens)], lambda s: o_res.at[:, cols(s, QW)]),
        (lambda to: dq_ref.at[cols(to, tokens)], lambda s: dq_res.at[:, cols(s, QW)]),
        (lambda to: grads.at[0, cols(to, tokens)], lambda s: dk_res.at[:, cols(s, D)]),
        (lambda to: grads.at[1, cols(to, tokens)], lambda s: dv_res.at[:, cols(s, D)]),
    )

    def at(kind, along, across):
        return across * SIDE + along if kind == 0 else along * SIDE + across

    def part(kind, to):
        if kind == 0:
            return send_ref.at[:, to, :, :D]
        return send_ref.at[to, :, :, D:]

    def share(kind, to, frm):
        return pltpu.make_async_remote_copy(
            part(kind, to), first.at[kind, frm], line_send.at[kind, to], line_recv.at[kind, frm],
            device_id=(at(kind, to, here[1 - kind]), head), device_id_type=MESH)

    def hold(kind):
        return pltpu.make_async_copy(part(kind, here[kind]), first.at[kind, here[kind]], local_sem.at[4 + kind])

    def push(kind, to, frm):
        return pltpu.make_async_remote_copy(
            sums.at[kind, to], second.at[kind, frm], push_send.at[kind, to], push_recv.at[kind, frm],
            device_id=(at(kind, here[kind], to), head), device_id_type=MESH)

    def send(a, to, frm):
        source, place = arrays[a]
        return pltpu.make_async_remote_copy(
            source(to), place(frm), head_send.at[a, to], head_recv.at[a, frm],
            device_id=(ctx, to), device_id_type=MESH)

    def keep(a):
        source, place = arrays[a]
        return pltpu.make_async_copy(source(head), place(head), local_sem.at[a])

    def each_head(arrays_used, act):
        def one(n, _):
            peer = lax.rem(head + n, HEADS)
            for a in arrays_used:
                act(a, peer)
            return 0
        lax.fori_loop(1, HEADS, one, 0)

    for n in (1, 3, 2):
        for kind in range(2):
            share(kind, lax.rem(here[kind] + n, SIDE), here[kind]).start()
    for kind in range(2):
        hold(kind).start()
    each_head((0, 1), lambda a, p: send(a, p, head).start())
    keep(0).start()
    keep(1).start()
    start_total = pltpu.make_async_copy(own_ref, total, local_sem.at[6])
    start_total.start()
    for kind in range(2):
        hold(kind).wait()
        for n in range(1, SIDE):
            peer = lax.rem(here[kind] + n, SIDE)
            share(kind, peer, peer).wait_recv()

    def add_line(n, _):
        for kind in range(2):
            to = lax.rem(here[1 - kind] + n, SIDE)
            target = at(kind, here[kind], to)
            for b in range(2):
                acc = jnp.zeros((T, D), f32)
                for along in range(SIDE):
                    source = at(kind, along, here[1 - kind])
                    take = jnp.logical_and(lists_block(lists, source, 2 * target + b), source != target)
                    acc += jnp.where(take, first[kind, along, to].astype(f32), 0.0)
                sums[kind, to, b] = acc.astype(bf)

            @pl.when(n < SIDE)
            def _():
                push(kind, to, here[1 - kind]).start()
        return 0

    lax.fori_loop(1, SIDE + 1, add_line, 0)
    start_total.wait()
    for kind in range(2):
        for b in range(2):
            total[kind, b] += sums[kind, here[1 - kind], b].astype(f32)
        for n in range(1, SIDE):
            frm = lax.rem(here[1 - kind] + n, SIDE)
            push(kind, frm, frm).wait_recv()
            for b in range(2):
                total[kind, b] += second[kind, frm, b].astype(f32)
        for b in range(2):
            grads[kind, b * T:(b + 1) * T] = total[kind, b].astype(bf)

    each_head((2, 3), lambda a, p: send(a, p, head).start())
    keep(2).start()
    keep(3).start()
    for kind in range(2):
        for n in range(1, SIDE):
            share(kind, lax.rem(here[kind] + n, SIDE), here[kind]).wait_send()
            push(kind, lax.rem(here[1 - kind] + n, SIDE), here[1 - kind]).wait_send()
    each_head(range(4), lambda a, p: send(a, p, head).wait_send())
    each_head(range(4), lambda a, p: send(a, p, p).wait_recv())
    for a in range(4):
        keep(a).wait()


def collect(lists, out, dq, send, own):
    f32, bf = jnp.float32, jnp.bfloat16
    any_spec = pl.BlockSpec(memory_space=pl.ANY)
    tokens = 2 * T // HEADS
    wide = jax.ShapeDtypeStruct((tokens, HEADS * QW), bf)
    thin = jax.ShapeDtypeStruct((tokens, HEADS * D), bf)
    dma = pltpu.SemaphoreType.DMA
    return pl.pallas_call(
        collect_kernel,
        out_shape=(wide, wide, thin, thin),
        in_specs=[pl.BlockSpec(memory_space=pltpu.SMEM)] + [any_spec] * 4,
        out_specs=(any_spec,) * 4,
        scratch_shapes=[
            pltpu.VMEM((2, SIDE, SIDE, T, D), bf),
            pltpu.VMEM((2, SIDE, 2, T, D), bf),
            pltpu.VMEM((2, SIDE, 2, T, D), bf),
            pltpu.VMEM((2, 2, T, D), f32),
            pltpu.VMEM((2, 2 * T, D), bf),
            dma((4, HEADS)), dma((4, HEADS)), dma((2, SIDE)), dma((2, SIDE)),
            dma((2, SIDE)), dma((2, SIDE)), dma((7,)),
        ],
        compiler_params=pltpu.CompilerParams(collective_id=1, has_side_effects=True, vmem_limit_bytes=60 * 2**20),
    )(lists, out, dq, send, own)


def shards(input_queries, input_keys, input_values, cotangent, block_list, block_count):
    queries, cot, table = spread(block_list, input_queries, input_keys, input_values, cotangent)
    out, dq, send, own = attn(block_list, block_count, queries, cot, table)
    return collect(block_list, out, dq, send.reshape(SIDE, SIDE, T, 2 * D), own)


def solution(mesh):
    spec = P(("ctx", "head"), None)
    return jax.shard_map(
        shards,
        mesh=mesh,
        in_specs=(spec,) * 4 + (P(), P()),
        out_specs=(spec,) * 4,
        check_vma=False,
    )
```

```python
import jax
import jax.numpy as jnp
from jax import lax
from jax.experimental import pallas as pl
from jax.experimental.pallas import tpu as pltpu
from jax.sharding import PartitionSpec as P

D = 128
T = 512
GROUP = 6
QW = GROUP * D
SIDE = 4
CTX = SIDE * SIDE
HEADS = 8
MOST = 8
SCALE = D**-0.5
LOG2E = 1.4426950408889634
NT = (((1,), (1,)), ((), ()))
MESH = pl.DeviceIdType.MESH


def attn_kernel(lists, counts, q_hbm, cot_hbm, kv_hbm, out_hbm, dq_hbm, send_hbm, own_hbm,
                q, cot, kv, weights, acc, dqa, stat, scaled_t, scaled, out, dq, send, own,
                kv_sem, in_sem, out_sem, send_sem):
    f32, bf = jnp.float32, jnp.bfloat16
    ctx = lax.axis_index("ctx")

    def owner(b, i):
        return lists[i, 2 * ctx + b] // 2

    def named(b, block_owner):
        hits = jnp.int32(0)
        for n in range(1, MOST):
            hits += (owner(b, n) == block_owner).astype(jnp.int32)
        return hits > 0

    def rows(b):
        return pl.ds(b * T, T)

    def fetch(b, i):
        slot = jnp.where(i == 0, CTX + b, owner(b, i))
        return pltpu.make_async_copy(kv_hbm.at[slot], kv.at[b * MOST + i], kv_sem.at[b * MOST + i])

    def load(b, a):
        source, place = ((q_hbm, q), (cot_hbm, cot))[a]
        return pltpu.make_async_copy(source.at[rows(b)], place.at[rows(b)], in_sem.at[b, a])

    def store(b, a):
        source, place = ((out, out_hbm), (dq, dq_hbm))[a]
        return pltpu.make_async_copy(source.at[rows(b)], place.at[rows(b)], out_sem.at[b, a])

    def store_own(b):
        return pltpu.make_async_copy(own.at[:, b], own_hbm.at[:, b], out_sem.at[b, 2])

    def store_send(d):
        return pltpu.make_async_copy(send.at[d], send_hbm.at[d], send_sem.at[d])

    def each_live(b, act, start=0):
        def one(i, _):
            act(i)
            return 0
        lax.fori_loop(start, counts[2 * ctx + b], one, 0)

    for b in range(2):
        load(b, 0).start()
        each_live(b, lambda i: fetch(b, i).start())
        load(b, 1).start()

    for b in range(2):
        lo = b * T

        def score(i, j):
            return lax.dot_general(kv[b * MOST + i, :, :D], q[lo:lo + T, j * D:(j + 1) * D], NT,
                                   preferred_element_type=f32)

        def top(i):
            for j in range(GROUP):
                best = jnp.max(score(i, j), axis=0, keepdims=True) * (SCALE * LOG2E)
                stat[0, j:j + 1] = jnp.maximum(stat[0, j:j + 1], best)

        def attend(i, shifted):
            values_t = kv[b * MOST + i, :, D:].T
            for j in range(GROUP):
                level = score(i, j) * (SCALE * LOG2E)
                if shifted:
                    level = level - stat[0, j:j + 1]
                weight = jnp.exp2(level)
                stat[1, j:j + 1] += jnp.sum(weight, axis=0, keepdims=True)
                weight = weight.astype(bf)
                weights[i, :, j * T:(j + 1) * T] = weight
                acc[j] += jnp.dot(values_t, weight, preferred_element_type=f32)

        def clear():
            acc[...] = jnp.zeros_like(acc)
            stat[1] = jnp.zeros((8, T), f32)

        def attend_first(i):
            fetch(b, i).wait()
            attend(i, False)

        load(b, 0).wait()
        clear()
        each_live(b, attend_first)
        sums = stat[1, :GROUP]
        safe = jnp.logical_and(jnp.min(sums) > 2.0**-60, jnp.max(sums) < 2.0**60)

        @pl.when(jnp.logical_not(safe))
        def _():
            stat[0] = jnp.full((8, T), -1e30, f32)
            each_live(b, top)
            clear()
            each_live(b, lambda i: attend(i, True))

        load(b, 1).wait()
        for j in range(GROUP):
            inverse = 1.0 / stat[1, j:j + 1]
            attended = (acc[j] * inverse).astype(bf)
            out[lo:lo + T, j * D:(j + 1) * D] = attended.T
            cot_t = cot[lo:lo + T, j * D:(j + 1) * D].T.astype(f32)
            stat[2, j:j + 1] = jnp.sum(attended.astype(f32) * cot_t, axis=0, keepdims=True) * inverse
            part = (cot_t * inverse).astype(bf)
            scaled_t[j] = part
            scaled[j] = part.T
        store(b, 0).start()
        dqa[...] = jnp.zeros_like(dqa)

        def back(i):
            keys = kv[b * MOST + i, :, :D]
            values = kv[b * MOST + i, :, D:]
            keys_t = keys.T
            dk = jnp.zeros((T, D), f32)
            dv = jnp.zeros((T, D), f32)
            for j in range(GROUP):
                change = jnp.dot(values, scaled_t[j], preferred_element_type=f32) - stat[2, j:j + 1]
                weight = weights[i, :, j * T:(j + 1) * T]
                ds = (weight.astype(f32) * change).astype(bf)
                dqa[j] += jnp.dot(keys_t, ds, preferred_element_type=f32)
                dk += jnp.dot(ds, q[lo:lo + T, j * D:(j + 1) * D], preferred_element_type=f32)
                dv += jnp.dot(weight, scaled[j], preferred_element_type=f32)
            dk = dk * SCALE
            d = owner(b, i)
            other = named(1 - b, d)

            @pl.when(i == 0)
            def _():
                own[0, b] = dk
                own[1, b] = dv

            if b == 0:
                @pl.when(i > 0)
                def _():
                    send[d, :, :D] = dk.astype(bf)
                    send[d, :, D:] = dv.astype(bf)

                @pl.when(jnp.logical_and(i > 0, jnp.logical_not(other)))
                def _():
                    store_send(d).start()
            else:
                @pl.when(jnp.logical_and(i > 0, jnp.logical_not(other)))
                def _():
                    send[d, :, :D] = dk.astype(bf)
                    send[d, :, D:] = dv.astype(bf)

                @pl.when(jnp.logical_and(i > 0, other))
                def _():
                    send[d, :, :D] = (send[d, :, :D].astype(f32) + dk).astype(bf)
                    send[d, :, D:] = (send[d, :, D:].astype(f32) + dv).astype(bf)

                @pl.when(i > 0)
                def _():
                    store_send(d).start()

        each_live(b, back)
        store_own(b).start()
        for j in range(GROUP):
            dq[lo:lo + T, j * D:(j + 1) * D] = (dqa[j] * SCALE).astype(bf).T
        store(b, 1).start()

    def end_first(i):
        d = owner(0, i)

        @pl.when(jnp.logical_not(named(1, d)))
        def _():
            store_send(d).wait()

    each_live(0, end_first, 1)
    each_live(1, lambda i: store_send(owner(1, i)).wait(), 1)
    for b in range(2):
        store(b, 0).wait()
        store(b, 1).wait()
        store_own(b).wait()


def attn(lists, counts, q, cot, kv):
    f32, bf = jnp.float32, jnp.bfloat16
    any_spec = pl.BlockSpec(memory_space=pl.ANY)
    dma = pltpu.SemaphoreType.DMA
    return pl.pallas_call(
        attn_kernel,
        out_shape=(jax.ShapeDtypeStruct((2 * T, QW), bf), jax.ShapeDtypeStruct((2 * T, QW), bf),
                   jax.ShapeDtypeStruct((CTX, T, 2 * D), bf), jax.ShapeDtypeStruct((2, 2, T, D), f32)),
        in_specs=[pl.BlockSpec(memory_space=pltpu.SMEM)] * 2 + [any_spec] * 3,
        out_specs=(any_spec,) * 4,
        scratch_shapes=[
            pltpu.VMEM((2 * T, QW), bf), pltpu.VMEM((2 * T, QW), bf), pltpu.VMEM((2 * MOST, T, 2 * D), bf),
            pltpu.VMEM((MOST, T, GROUP * T), bf), pltpu.VMEM((GROUP, D, T), f32), pltpu.VMEM((GROUP, D, T), f32),
            pltpu.VMEM((3, 8, T), f32), pltpu.VMEM((GROUP, D, T), bf), pltpu.VMEM((GROUP, T, D), bf),
            pltpu.VMEM((2 * T, QW), bf), pltpu.VMEM((2 * T, QW), bf), pltpu.VMEM((CTX, T, 2 * D), bf),
            pltpu.VMEM((2, 2, T, D), f32),
            dma((2 * MOST,)), dma((2, 2)), dma((2, 3)), dma((CTX,)),
        ],
        compiler_params=pltpu.CompilerParams(vmem_limit_bytes=62 * 2**20),
    )(lists, counts, q, cot, kv)


def greet(ctx, head):
    barrier = pltpu.get_barrier_semaphore()
    y, x = ctx // SIDE, lax.rem(ctx, SIDE)

    def line(n, _):
        pl.semaphore_signal(barrier, inc=1, device_id=(y * SIDE + lax.rem(x + n, SIDE), head), device_id_type=MESH)
        pl.semaphore_signal(barrier, inc=1, device_id=(lax.rem(y + n, SIDE) * SIDE + x, head), device_id_type=MESH)
        return 0

    def head_peer(n, _):
        pl.semaphore_signal(barrier, inc=1, device_id=(ctx, lax.rem(head + n, HEADS)), device_id_type=MESH)
        return 0

    lax.fori_loop(1, SIDE, line, 0)
    lax.fori_loop(1, HEADS, head_peer, 0)
    pl.semaphore_wait(barrier, 2 * (SIDE - 1) + HEADS - 1)


def cols(index, width):
    return pl.ds(pl.multiple_of(index * width, width), width)


def lists_block(lists, ctx, block):
    hits = jnp.int32(0)
    for b in range(2):
        for i in range(1, MOST):
            hits += (lists[i, 2 * ctx + b] == block).astype(jnp.int32)
    return hits > 0


def spread_kernel(lists, q_ref, k_ref, v_ref, c_ref, qh_ref, ch_ref, table_ref,
                  lines, stage, head_send, head_recv, line_send, line_recv, push_send, push_recv, local_sem, fill_sem):
    ctx, head = lax.axis_index("ctx"), lax.axis_index("head")
    y, x = ctx // SIDE, lax.rem(ctx, SIDE)
    here = (x, y)
    greet(ctx, head)
    tokens = k_ref.shape[0]
    arrays = (
        (k_ref, lambda s: lines.at[0, x, cols(s, tokens)], D),
        (v_ref, lambda s: lines.at[1, y, cols(s, tokens)], D),
        (q_ref, lambda s: qh_ref.at[cols(s, tokens)], QW),
        (c_ref, lambda s: ch_ref.at[cols(s, tokens)], QW),
    )

    def at(kind, along, across):
        return across * SIDE + along if kind == 0 else along * SIDE + across

    def send(a, to, frm):
        ref, place, width = arrays[a]
        return pltpu.make_async_remote_copy(
            ref.at[:, cols(to, width)], place(frm), head_send.at[a, to], head_recv.at[a, frm],
            device_id=(ctx, to), device_id_type=MESH)

    def keep(a):
        ref, place, width = arrays[a]
        return pltpu.make_async_copy(ref.at[:, cols(head, width)], place(head), local_sem.at[a])

    def each_head(arrays_used, act):
        def one(n, _):
            peer = lax.rem(head + n, HEADS)
            for a in arrays_used:
                act(a, peer)
            return 0
        lax.fori_loop(1, HEADS, one, 0)

    for a in range(4):
        keep(a).start()
    each_head((0, 1), lambda a, p: send(a, p, head).start())
    each_head((2, 3), lambda a, p: send(a, p, head).start())
    keep(0).wait()
    keep(1).wait()
    each_head((0, 1), lambda a, p: send(a, p, p).wait_recv())

    def share(kind, to, frm):
        return pltpu.make_async_remote_copy(
            lines.at[kind, frm], lines.at[kind, frm], line_send.at[kind, to], line_recv.at[kind, frm],
            device_id=(at(kind, to, here[1 - kind]), head), device_id_type=MESH)

    def push(kind, to, along, frm):
        source = at(kind, along, frm)
        return pltpu.make_async_remote_copy(
            stage.at[kind, to, along], table_ref.at[source, :, kind * D:(kind + 1) * D],
            push_send.at[kind, to, along], push_recv.at[kind, frm, along],
            device_id=(at(kind, here[kind], to), head), device_id_type=MESH)

    def fill(kind, along):
        mine = here[1 - kind]
        return pltpu.make_async_copy(
            stage.at[kind, mine, along], table_ref.at[at(kind, along, mine), :, kind * D:(kind + 1) * D],
            fill_sem.at[kind, along])

    def own(kind, b):
        return pltpu.make_async_copy(
            lines.at[kind, here[kind], b * T:(b + 1) * T], table_ref.at[CTX + b, :, kind * D:(kind + 1) * D],
            local_sem.at[4 + 2 * kind + b])

    def prepare(kind, to, along):
        source = at(kind, along, here[1 - kind])
        second = lists_block(lists, at(kind, here[kind], to), 2 * source + 1)
        stage[kind, to, along] = jnp.where(second, lines[kind, along, T:], lines[kind, along, :T])

    for n in (1, 3, 2):
        for kind in range(2):
            share(kind, lax.rem(here[kind] + n, SIDE), here[kind]).start()
    for kind in range(2):
        for b in range(2):
            own(kind, b).start()

    def push_all(m, _):
        for kind in range(2):
            along = lax.rem(here[kind] + m, SIDE)

            @pl.when(m > 0)
            def _():
                share(kind, along, along).wait_recv()

            for n in range(1, SIDE):
                to = lax.rem(here[1 - kind] + n, SIDE)
                prepare(kind, to, along)
                push(kind, to, along, here[1 - kind]).start()

            @pl.when(m > 0)
            def _():
                prepare(kind, here[1 - kind], along)
                fill(kind, along).start()
        return 0

    lax.fori_loop(0, SIDE, push_all, 0)

    each_head(range(4), lambda a, p: send(a, p, head).wait_send())
    each_head((2, 3), lambda a, p: send(a, p, p).wait_recv())
    keep(2).wait()
    keep(3).wait()

    def drain(m, _):
        for kind in range(2):
            along = lax.rem(here[kind] + m, SIDE)

            @pl.when(m > 0)
            def _():
                share(kind, along, here[kind]).wait_send()
                fill(kind, along).wait()

            for n in range(1, SIDE):
                peer = lax.rem(here[1 - kind] + n, SIDE)
                push(kind, peer, along, here[1 - kind]).wait_send()
                push(kind, peer, along, peer).wait_recv()
        return 0

    lax.fori_loop(0, SIDE, drain, 0)
    for kind in range(2):
        for b in range(2):
            own(kind, b).wait()


def spread(lists, q, k, v, cot):
    bf = jnp.bfloat16
    any_spec = pl.BlockSpec(memory_space=pl.ANY)
    dma = pltpu.SemaphoreType.DMA
    return pl.pallas_call(
        spread_kernel,
        out_shape=(jax.ShapeDtypeStruct((2 * T, QW), bf), jax.ShapeDtypeStruct((2 * T, QW), bf),
                   jax.ShapeDtypeStruct((CTX + 2, T, 2 * D), bf)),
        in_specs=[pl.BlockSpec(memory_space=pltpu.SMEM)] + [any_spec] * 4,
        out_specs=(any_spec,) * 3,
        scratch_shapes=[
            pltpu.VMEM((2, SIDE, 2 * T, D), bf),
            pltpu.VMEM((2, SIDE, SIDE, T, D), bf),
            dma((4, HEADS)), dma((4, HEADS)), dma((2, SIDE)), dma((2, SIDE)),
            dma((2, SIDE, SIDE)), dma((2, SIDE, SIDE)), dma((8,)), dma((2, SIDE)),
        ],
        compiler_params=pltpu.CompilerParams(collective_id=0, has_side_effects=True, vmem_limit_bytes=60 * 2**20),
    )(lists, q, k, v, cot)


def collect_kernel(lists, out_ref, dq_ref, send_ref, own_ref, o_res, dq_res, dk_res, dv_res,
                   first, sums, second, total, grads,
                   head_send, head_recv, line_send, line_recv, push_send, push_recv, local_sem):
    f32, bf = jnp.float32, jnp.bfloat16
    ctx, head = lax.axis_index("ctx"), lax.axis_index("head")
    y, x = ctx // SIDE, lax.rem(ctx, SIDE)
    here = (x, y)
    greet(ctx, head)
    tokens = o_res.shape[0]
    arrays = (
        (lambda to: out_ref.at[cols(to, tokens)], lambda s: o_res.at[:, cols(s, QW)]),
        (lambda to: dq_ref.at[cols(to, tokens)], lambda s: dq_res.at[:, cols(s, QW)]),
        (lambda to: grads.at[0, cols(to, tokens)], lambda s: dk_res.at[:, cols(s, D)]),
        (lambda to: grads.at[1, cols(to, tokens)], lambda s: dv_res.at[:, cols(s, D)]),
    )

    def at(kind, along, across):
        return across * SIDE + along if kind == 0 else along * SIDE + across

    def part(kind, to):
        if kind == 0:
            return send_ref.at[:, to, :, :D]
        return send_ref.at[to, :, :, D:]

    def share(kind, to, frm):
        return pltpu.make_async_remote_copy(
            part(kind, to), first.at[kind, frm], line_send.at[kind, to], line_recv.at[kind, frm],
            device_id=(at(kind, to, here[1 - kind]), head), device_id_type=MESH)

    def hold(kind):
        return pltpu.make_async_copy(part(kind, here[kind]), first.at[kind, here[kind]], local_sem.at[4 + kind])

    def push(kind, to, frm):
        return pltpu.make_async_remote_copy(
            sums.at[kind, to], second.at[kind, frm], push_send.at[kind, to], push_recv.at[kind, frm],
            device_id=(at(kind, here[kind], to), head), device_id_type=MESH)

    def send(a, to, frm):
        source, place = arrays[a]
        return pltpu.make_async_remote_copy(
            source(to), place(frm), head_send.at[a, to], head_recv.at[a, frm],
            device_id=(ctx, to), device_id_type=MESH)

    def keep(a):
        source, place = arrays[a]
        return pltpu.make_async_copy(source(head), place(head), local_sem.at[a])

    def each_head(arrays_used, act):
        def one(n, _):
            peer = lax.rem(head + n, HEADS)
            for a in arrays_used:
                act(a, peer)
            return 0
        lax.fori_loop(1, HEADS, one, 0)

    for n in (1, 3, 2):
        for kind in range(2):
            share(kind, lax.rem(here[kind] + n, SIDE), here[kind]).start()
    for kind in range(2):
        hold(kind).start()
    each_head((0, 1), lambda a, p: send(a, p, head).start())
    keep(0).start()
    keep(1).start()
    start_total = pltpu.make_async_copy(own_ref, total, local_sem.at[6])
    start_total.start()
    for kind in range(2):
        hold(kind).wait()
        for n in range(1, SIDE):
            peer = lax.rem(here[kind] + n, SIDE)
            share(kind, peer, peer).wait_recv()

    def add_line(n, _):
        for kind in range(2):
            to = lax.rem(here[1 - kind] + n, SIDE)
            target = at(kind, here[kind], to)
            for b in range(2):
                acc = jnp.zeros((T, D), f32)
                for along in range(SIDE):
                    source = at(kind, along, here[1 - kind])
                    take = jnp.logical_and(lists_block(lists, source, 2 * target + b), source != target)
                    acc += jnp.where(take, first[kind, along, to].astype(f32), 0.0)
                sums[kind, to, b] = acc.astype(bf)

            @pl.when(n < SIDE)
            def _():
                push(kind, to, here[1 - kind]).start()
        return 0

    lax.fori_loop(1, SIDE + 1, add_line, 0)
    start_total.wait()
    for kind in range(2):
        for b in range(2):
            total[kind, b] += sums[kind, here[1 - kind], b].astype(f32)
        for n in range(1, SIDE):
            frm = lax.rem(here[1 - kind] + n, SIDE)
            push(kind, frm, frm).wait_recv()
            for b in range(2):
                total[kind, b] += second[kind, frm, b].astype(f32)
        for b in range(2):
            grads[kind, b * T:(b + 1) * T] = total[kind, b].astype(bf)

    each_head((2, 3), lambda a, p: send(a, p, head).start())
    keep(2).start()
    keep(3).start()
    for kind in range(2):
        for n in range(1, SIDE):
            share(kind, lax.rem(here[kind] + n, SIDE), here[kind]).wait_send()
            push(kind, lax.rem(here[1 - kind] + n, SIDE), here[1 - kind]).wait_send()
    each_head(range(4), lambda a, p: send(a, p, head).wait_send())
    each_head(range(4), lambda a, p: send(a, p, p).wait_recv())
    for a in range(4):
        keep(a).wait()


def collect(lists, out, dq, send, own):
    f32, bf = jnp.float32, jnp.bfloat16
    any_spec = pl.BlockSpec(memory_space=pl.ANY)
    tokens = 2 * T // HEADS
    wide = jax.ShapeDtypeStruct((tokens, HEADS * QW), bf)
    thin = jax.ShapeDtypeStruct((tokens, HEADS * D), bf)
    dma = pltpu.SemaphoreType.DMA
    return pl.pallas_call(
        collect_kernel,
        out_shape=(wide, wide, thin, thin),
        in_specs=[pl.BlockSpec(memory_space=pltpu.SMEM)] + [any_spec] * 4,
        out_specs=(any_spec,) * 4,
        scratch_shapes=[
            pltpu.VMEM((2, SIDE, SIDE, T, D), bf),
            pltpu.VMEM((2, SIDE, 2, T, D), bf),
            pltpu.VMEM((2, SIDE, 2, T, D), bf),
            pltpu.VMEM((2, 2, T, D), f32),
            pltpu.VMEM((2, 2 * T, D), bf),
            dma((4, HEADS)), dma((4, HEADS)), dma((2, SIDE)), dma((2, SIDE)),
            dma((2, SIDE)), dma((2, SIDE)), dma((7,)),
        ],
        compiler_params=pltpu.CompilerParams(collective_id=1, has_side_effects=True, vmem_limit_bytes=60 * 2**20),
    )(lists, out, dq, send, own)


def shards(input_queries, input_keys, input_values, cotangent, block_list, block_count):
    lists = block_list.T
    queries, cot, table = spread(lists, input_queries, input_keys, input_values, cotangent)
    out, dq, send, own = attn(lists, block_count, queries, cot, table)
    return collect(lists, out, dq, send.reshape(SIDE, SIDE, T, 2 * D), own)


def solution(mesh):
    spec = P(("ctx", "head"), None)
    return jax.shard_map(
        shards,
        mesh=mesh,
        in_specs=(spec,) * 4 + (P(), P()),
        out_specs=(spec,) * 4,
        check_vma=False,
    )
```

```python
import jax
import jax.numpy as jnp
from jax import lax
from jax.experimental import pallas as pl
from jax.experimental.pallas import tpu as pltpu
from jax.sharding import PartitionSpec as P

D = 128
T = 512
GROUP = 6
QW = GROUP * D
SIDE = 4
CTX = SIDE * SIDE
HEADS = 8
MOST = 8
SCALE = D**-0.5
LOG2E = 1.4426950408889634
NT = (((1,), (1,)), ((), ()))
MESH = pl.DeviceIdType.MESH


def attn_kernel(lists, counts, q_hbm, cot_hbm, kv_hbm, out_hbm, dq_hbm, send_hbm, own_hbm,
                q, cot, kv, weights, acc, dqa, stat, scaled_t, scaled, out, dq, send, own,
                dscore, qs, kv_sem, in_sem, out_sem, send_sem):
    f32, bf = jnp.float32, jnp.bfloat16
    ctx = lax.axis_index("ctx")

    def owner(b, i):
        return lists[i, 2 * ctx + b] // 2

    def named(b, block_owner):
        hits = jnp.int32(0)
        for n in range(1, MOST):
            hits += (owner(b, n) == block_owner).astype(jnp.int32)
        return hits > 0

    def rows(b):
        return pl.ds(b * T, T)

    def fetch(b, i):
        slot = jnp.where(i == 0, CTX + b, owner(b, i))
        return pltpu.make_async_copy(kv_hbm.at[slot], kv.at[b * MOST + i], kv_sem.at[b * MOST + i])

    def load(b, a):
        source, place = ((q_hbm, q), (cot_hbm, cot))[a]
        return pltpu.make_async_copy(source.at[rows(b)], place.at[rows(b)], in_sem.at[b, a])

    def store(b, a):
        source, place = ((out, out_hbm), (dq, dq_hbm))[a]
        return pltpu.make_async_copy(source.at[rows(b)], place.at[rows(b)], out_sem.at[b, a])

    def store_own(b):
        return pltpu.make_async_copy(own.at[:, b], own_hbm.at[:, b], out_sem.at[b, 2])

    def store_send(d):
        return pltpu.make_async_copy(send.at[d], send_hbm.at[d], send_sem.at[d])

    def each_live(b, act, start=0):
        def one(i, _):
            act(i)
            return 0
        lax.fori_loop(start, counts[2 * ctx + b], one, 0)

    for b in range(2):
        load(b, 0).start()
        each_live(b, lambda i: fetch(b, i).start())
        load(b, 1).start()

    for b in range(2):
        lo = b * T

        def score(i, j):
            return lax.dot_general(kv[b * MOST + i, :, :D], q[lo:lo + T, j * D:(j + 1) * D], NT,
                                   preferred_element_type=f32)

        def top(i):
            for j in range(GROUP):
                best = jnp.max(score(i, j), axis=0, keepdims=True) * (SCALE * LOG2E)
                stat[0, j:j + 1] = jnp.maximum(stat[0, j:j + 1], best)

        def attend(i, shifted):
            values_t = kv[b * MOST + i, :, D:].T
            for j in range(GROUP):
                level = score(i, j) * (SCALE * LOG2E)
                if shifted:
                    level = level - stat[0, j:j + 1]
                weight = jnp.exp2(level)
                stat[1, j:j + 1] += jnp.sum(weight, axis=0, keepdims=True)
                weights[i, :, j * T:(j + 1) * T] = weight.astype(bf)
            for j in range(GROUP):
                acc[j] += jnp.dot(values_t, weights[i, :, j * T:(j + 1) * T], preferred_element_type=f32)

        def clear():
            acc[...] = jnp.zeros_like(acc)
            stat[1] = jnp.zeros((8, T), f32)

        def attend_first(i):
            fetch(b, i).wait()
            attend(i, False)

        load(b, 0).wait()
        clear()
        each_live(b, attend_first)
        sums = stat[1, :GROUP]
        safe = jnp.logical_and(jnp.min(sums) > 2.0**-60, jnp.max(sums) < 2.0**60)

        @pl.when(jnp.logical_not(safe))
        def _():
            stat[0] = jnp.full((8, T), -1e30, f32)
            each_live(b, top)
            clear()
            each_live(b, lambda i: attend(i, True))

        load(b, 1).wait()
        for j in range(GROUP):
            inverse = 1.0 / stat[1, j:j + 1]
            attended = (acc[j] * inverse).astype(bf)
            out[lo:lo + T, j * D:(j + 1) * D] = attended.T
            cot_t = cot[lo:lo + T, j * D:(j + 1) * D].T.astype(f32)
            stat[2, j:j + 1] = jnp.sum(attended.astype(f32) * cot_t, axis=0, keepdims=True) * inverse
            part = (cot_t * inverse).astype(bf)
            scaled_t[j] = part
            scaled[j] = part.T
        store(b, 0).start()
        dqa[...] = jnp.zeros_like(dqa)
        for j in range(GROUP):
            qs[j * T:(j + 1) * T] = q[lo:lo + T, j * D:(j + 1) * D]

        def back(i):
            keys = kv[b * MOST + i, :, :D]
            values = kv[b * MOST + i, :, D:]
            keys_t = keys.T
            dk = jnp.zeros((T, D), f32)
            dv = jnp.zeros((T, D), f32)
            for j in range(GROUP):
                change = jnp.dot(values, scaled_t[j], preferred_element_type=f32) - stat[2, j:j + 1]
                weight = weights[i, :, j * T:(j + 1) * T]
                dscore[:, j * T:(j + 1) * T] = (weight.astype(f32) * change).astype(bf)
            for j in range(GROUP):
                dqa[j] += jnp.dot(keys_t, dscore[:, j * T:(j + 1) * T], preferred_element_type=f32)
            dv = jnp.dot(weights[i], scaled[...].reshape(GROUP * T, D), preferred_element_type=f32)
            dk = jnp.dot(dscore[...], qs[...], preferred_element_type=f32)
            dk = dk * SCALE
            d = owner(b, i)
            other = named(1 - b, d)

            @pl.when(i == 0)
            def _():
                own[0, b] = dk
                own[1, b] = dv

            if b == 0:
                @pl.when(i > 0)
                def _():
                    send[d, :, :D] = dk.astype(bf)
                    send[d, :, D:] = dv.astype(bf)

                @pl.when(jnp.logical_and(i > 0, jnp.logical_not(other)))
                def _():
                    store_send(d).start()
            else:
                @pl.when(jnp.logical_and(i > 0, jnp.logical_not(other)))
                def _():
                    send[d, :, :D] = dk.astype(bf)
                    send[d, :, D:] = dv.astype(bf)

                @pl.when(jnp.logical_and(i > 0, other))
                def _():
                    send[d, :, :D] = (send[d, :, :D].astype(f32) + dk).astype(bf)
                    send[d, :, D:] = (send[d, :, D:].astype(f32) + dv).astype(bf)

                @pl.when(i > 0)
                def _():
                    store_send(d).start()

        each_live(b, back)
        store_own(b).start()
        for j in range(GROUP):
            dq[lo:lo + T, j * D:(j + 1) * D] = (dqa[j] * SCALE).astype(bf).T
        store(b, 1).start()

    def end_first(i):
        d = owner(0, i)

        @pl.when(jnp.logical_not(named(1, d)))
        def _():
            store_send(d).wait()

    each_live(0, end_first, 1)
    each_live(1, lambda i: store_send(owner(1, i)).wait(), 1)
    for b in range(2):
        store(b, 0).wait()
        store(b, 1).wait()
        store_own(b).wait()


def attn(lists, counts, q, cot, kv):
    f32, bf = jnp.float32, jnp.bfloat16
    any_spec = pl.BlockSpec(memory_space=pl.ANY)
    dma = pltpu.SemaphoreType.DMA
    return pl.pallas_call(
        attn_kernel,
        out_shape=(jax.ShapeDtypeStruct((2 * T, QW), bf), jax.ShapeDtypeStruct((2 * T, QW), bf),
                   jax.ShapeDtypeStruct((CTX, T, 2 * D), bf), jax.ShapeDtypeStruct((2, 2, T, D), f32)),
        in_specs=[pl.BlockSpec(memory_space=pltpu.SMEM)] * 2 + [any_spec] * 3,
        out_specs=(any_spec,) * 4,
        scratch_shapes=[
            pltpu.VMEM((2 * T, QW), bf), pltpu.VMEM((2 * T, QW), bf), pltpu.VMEM((2 * MOST, T, 2 * D), bf),
            pltpu.VMEM((MOST, T, GROUP * T), bf), pltpu.VMEM((GROUP, D, T), f32), pltpu.VMEM((GROUP, D, T), f32),
            pltpu.VMEM((3, 8, T), f32), pltpu.VMEM((GROUP, D, T), bf), pltpu.VMEM((GROUP, T, D), bf),
            pltpu.VMEM((2 * T, QW), bf), pltpu.VMEM((2 * T, QW), bf), pltpu.VMEM((CTX, T, 2 * D), bf),
            pltpu.VMEM((2, 2, T, D), f32),
            pltpu.VMEM((T, GROUP * T), bf), pltpu.VMEM((GROUP * T, D), bf),
            dma((2 * MOST,)), dma((2, 2)), dma((2, 3)), dma((CTX,)),
        ],
        compiler_params=pltpu.CompilerParams(vmem_limit_bytes=62 * 2**20),
    )(lists, counts, q, cot, kv)


def greet(ctx, head):
    barrier = pltpu.get_barrier_semaphore()
    y, x = ctx // SIDE, lax.rem(ctx, SIDE)

    def line(n, _):
        pl.semaphore_signal(barrier, inc=1, device_id=(y * SIDE + lax.rem(x + n, SIDE), head), device_id_type=MESH)
        pl.semaphore_signal(barrier, inc=1, device_id=(lax.rem(y + n, SIDE) * SIDE + x, head), device_id_type=MESH)
        return 0

    def head_peer(n, _):
        pl.semaphore_signal(barrier, inc=1, device_id=(ctx, lax.rem(head + n, HEADS)), device_id_type=MESH)
        return 0

    lax.fori_loop(1, SIDE, line, 0)
    lax.fori_loop(1, HEADS, head_peer, 0)
    pl.semaphore_wait(barrier, 2 * (SIDE - 1) + HEADS - 1)


def cols(index, width):
    return pl.ds(pl.multiple_of(index * width, width), width)


def lists_block(lists, ctx, block):
    hits = jnp.int32(0)
    for b in range(2):
        for i in range(1, MOST):
            hits += (lists[i, 2 * ctx + b] == block).astype(jnp.int32)
    return hits > 0


def spread_kernel(lists, q_ref, k_ref, v_ref, c_ref, qh_ref, ch_ref, table_ref,
                  lines, stage, head_send, head_recv, line_send, line_recv, push_send, push_recv, local_sem, fill_sem):
    ctx, head = lax.axis_index("ctx"), lax.axis_index("head")
    y, x = ctx // SIDE, lax.rem(ctx, SIDE)
    here = (x, y)
    greet(ctx, head)
    tokens = k_ref.shape[0]
    arrays = (
        (k_ref, lambda s: lines.at[0, x, cols(s, tokens)], D),
        (v_ref, lambda s: lines.at[1, y, cols(s, tokens)], D),
        (q_ref, lambda s: qh_ref.at[cols(s, tokens)], QW),
        (c_ref, lambda s: ch_ref.at[cols(s, tokens)], QW),
    )

    def at(kind, along, across):
        return across * SIDE + along if kind == 0 else along * SIDE + across

    def send(a, to, frm):
        ref, place, width = arrays[a]
        return pltpu.make_async_remote_copy(
            ref.at[:, cols(to, width)], place(frm), head_send.at[a, to], head_recv.at[a, frm],
            device_id=(ctx, to), device_id_type=MESH)

    def keep(a):
        ref, place, width = arrays[a]
        return pltpu.make_async_copy(ref.at[:, cols(head, width)], place(head), local_sem.at[a])

    def each_head(arrays_used, act):
        def one(n, _):
            peer = lax.rem(head + n, HEADS)
            for a in arrays_used:
                act(a, peer)
            return 0
        lax.fori_loop(1, HEADS, one, 0)

    for a in range(4):
        keep(a).start()
    each_head((0, 1), lambda a, p: send(a, p, head).start())
    each_head((2, 3), lambda a, p: send(a, p, head).start())
    keep(0).wait()
    keep(1).wait()
    each_head((0, 1), lambda a, p: send(a, p, p).wait_recv())

    def share(kind, to, frm):
        return pltpu.make_async_remote_copy(
            lines.at[kind, frm], lines.at[kind, frm], line_send.at[kind, to], line_recv.at[kind, frm],
            device_id=(at(kind, to, here[1 - kind]), head), device_id_type=MESH)

    def push(kind, to, along, frm):
        source = at(kind, along, frm)
        return pltpu.make_async_remote_copy(
            stage.at[kind, to, along], table_ref.at[source, :, kind * D:(kind + 1) * D],
            push_send.at[kind, to, along], push_recv.at[kind, frm, along],
            device_id=(at(kind, here[kind], to), head), device_id_type=MESH)

    def fill(kind, along):
        mine = here[1 - kind]
        return pltpu.make_async_copy(
            stage.at[kind, mine, along], table_ref.at[at(kind, along, mine), :, kind * D:(kind + 1) * D],
            fill_sem.at[kind, along])

    def own(kind, b):
        return pltpu.make_async_copy(
            lines.at[kind, here[kind], b * T:(b + 1) * T], table_ref.at[CTX + b, :, kind * D:(kind + 1) * D],
            local_sem.at[4 + 2 * kind + b])

    def prepare(kind, to, along):
        source = at(kind, along, here[1 - kind])
        second = lists_block(lists, at(kind, here[kind], to), 2 * source + 1)
        stage[kind, to, along] = jnp.where(second, lines[kind, along, T:], lines[kind, along, :T])

    for n in (1, 3, 2):
        for kind in range(2):
            share(kind, lax.rem(here[kind] + n, SIDE), here[kind]).start()
    for kind in range(2):
        for b in range(2):
            own(kind, b).start()

    def push_all(m, _):
        for kind in range(2):
            along = lax.rem(here[kind] + m, SIDE)

            @pl.when(m > 0)
            def _():
                share(kind, along, along).wait_recv()

            for n in range(1, SIDE):
                to = lax.rem(here[1 - kind] + n, SIDE)
                prepare(kind, to, along)
                push(kind, to, along, here[1 - kind]).start()

            @pl.when(m > 0)
            def _():
                prepare(kind, here[1 - kind], along)
                fill(kind, along).start()
        return 0

    lax.fori_loop(0, SIDE, push_all, 0)

    each_head(range(4), lambda a, p: send(a, p, head).wait_send())
    each_head((2, 3), lambda a, p: send(a, p, p).wait_recv())
    keep(2).wait()
    keep(3).wait()

    def drain(m, _):
        for kind in range(2):
            along = lax.rem(here[kind] + m, SIDE)

            @pl.when(m > 0)
            def _():
                share(kind, along, here[kind]).wait_send()
                fill(kind, along).wait()

            for n in range(1, SIDE):
                peer = lax.rem(here[1 - kind] + n, SIDE)
                push(kind, peer, along, here[1 - kind]).wait_send()
                push(kind, peer, along, peer).wait_recv()
        return 0

    lax.fori_loop(0, SIDE, drain, 0)
    for kind in range(2):
        for b in range(2):
            own(kind, b).wait()


def spread(lists, q, k, v, cot):
    bf = jnp.bfloat16
    any_spec = pl.BlockSpec(memory_space=pl.ANY)
    dma = pltpu.SemaphoreType.DMA
    return pl.pallas_call(
        spread_kernel,
        out_shape=(jax.ShapeDtypeStruct((2 * T, QW), bf), jax.ShapeDtypeStruct((2 * T, QW), bf),
                   jax.ShapeDtypeStruct((CTX + 2, T, 2 * D), bf)),
        in_specs=[pl.BlockSpec(memory_space=pltpu.SMEM)] + [any_spec] * 4,
        out_specs=(any_spec,) * 3,
        scratch_shapes=[
            pltpu.VMEM((2, SIDE, 2 * T, D), bf),
            pltpu.VMEM((2, SIDE, SIDE, T, D), bf),
            dma((4, HEADS)), dma((4, HEADS)), dma((2, SIDE)), dma((2, SIDE)),
            dma((2, SIDE, SIDE)), dma((2, SIDE, SIDE)), dma((8,)), dma((2, SIDE)),
        ],
        compiler_params=pltpu.CompilerParams(collective_id=0, has_side_effects=True, vmem_limit_bytes=60 * 2**20),
    )(lists, q, k, v, cot)


def collect_kernel(lists, out_ref, dq_ref, send_ref, own_ref, o_res, dq_res, dk_res, dv_res,
                   first, sums, second, total, grads,
                   head_send, head_recv, line_send, line_recv, push_send, push_recv, local_sem):
    f32, bf = jnp.float32, jnp.bfloat16
    ctx, head = lax.axis_index("ctx"), lax.axis_index("head")
    y, x = ctx // SIDE, lax.rem(ctx, SIDE)
    here = (x, y)
    greet(ctx, head)
    tokens = o_res.shape[0]
    arrays = (
        (lambda to: out_ref.at[cols(to, tokens)], lambda s: o_res.at[:, cols(s, QW)]),
        (lambda to: dq_ref.at[cols(to, tokens)], lambda s: dq_res.at[:, cols(s, QW)]),
        (lambda to: grads.at[0, cols(to, tokens)], lambda s: dk_res.at[:, cols(s, D)]),
        (lambda to: grads.at[1, cols(to, tokens)], lambda s: dv_res.at[:, cols(s, D)]),
    )

    def at(kind, along, across):
        return across * SIDE + along if kind == 0 else along * SIDE + across

    def part(kind, to):
        if kind == 0:
            return send_ref.at[:, to, :, :D]
        return send_ref.at[to, :, :, D:]

    def share(kind, to, frm):
        return pltpu.make_async_remote_copy(
            part(kind, to), first.at[kind, frm], line_send.at[kind, to], line_recv.at[kind, frm],
            device_id=(at(kind, to, here[1 - kind]), head), device_id_type=MESH)

    def hold(kind):
        return pltpu.make_async_copy(part(kind, here[kind]), first.at[kind, here[kind]], local_sem.at[4 + kind])

    def push(kind, to, frm):
        return pltpu.make_async_remote_copy(
            sums.at[kind, to], second.at[kind, frm], push_send.at[kind, to], push_recv.at[kind, frm],
            device_id=(at(kind, here[kind], to), head), device_id_type=MESH)

    def send(a, to, frm):
        source, place = arrays[a]
        return pltpu.make_async_remote_copy(
            source(to), place(frm), head_send.at[a, to], head_recv.at[a, frm],
            device_id=(ctx, to), device_id_type=MESH)

    def keep(a):
        source, place = arrays[a]
        return pltpu.make_async_copy(source(head), place(head), local_sem.at[a])

    def each_head(arrays_used, act):
        def one(n, _):
            peer = lax.rem(head + n, HEADS)
            for a in arrays_used:
                act(a, peer)
            return 0
        lax.fori_loop(1, HEADS, one, 0)

    for n in (1, 3, 2):
        for kind in range(2):
            share(kind, lax.rem(here[kind] + n, SIDE), here[kind]).start()
    for kind in range(2):
        hold(kind).start()
    each_head((0, 1), lambda a, p: send(a, p, head).start())
    keep(0).start()
    keep(1).start()
    start_total = pltpu.make_async_copy(own_ref, total, local_sem.at[6])
    start_total.start()
    for kind in range(2):
        hold(kind).wait()
        for n in range(1, SIDE):
            peer = lax.rem(here[kind] + n, SIDE)
            share(kind, peer, peer).wait_recv()

    def add_line(n, _):
        for kind in range(2):
            to = lax.rem(here[1 - kind] + n, SIDE)
            target = at(kind, here[kind], to)
            for b in range(2):
                acc = jnp.zeros((T, D), f32)
                for along in range(SIDE):
                    source = at(kind, along, here[1 - kind])
                    take = jnp.logical_and(lists_block(lists, source, 2 * target + b), source != target)
                    acc += jnp.where(take, first[kind, along, to].astype(f32), 0.0)
                sums[kind, to, b] = acc.astype(bf)

            @pl.when(n < SIDE)
            def _():
                push(kind, to, here[1 - kind]).start()
        return 0

    lax.fori_loop(1, SIDE + 1, add_line, 0)
    start_total.wait()
    for kind in range(2):
        for b in range(2):
            total[kind, b] += sums[kind, here[1 - kind], b].astype(f32)
        for n in range(1, SIDE):
            frm = lax.rem(here[1 - kind] + n, SIDE)
            push(kind, frm, frm).wait_recv()
            for b in range(2):
                total[kind, b] += second[kind, frm, b].astype(f32)
        for b in range(2):
            grads[kind, b * T:(b + 1) * T] = total[kind, b].astype(bf)

    each_head((2, 3), lambda a, p: send(a, p, head).start())
    keep(2).start()
    keep(3).start()
    for kind in range(2):
        for n in range(1, SIDE):
            share(kind, lax.rem(here[kind] + n, SIDE), here[kind]).wait_send()
            push(kind, lax.rem(here[1 - kind] + n, SIDE), here[1 - kind]).wait_send()
    each_head(range(4), lambda a, p: send(a, p, head).wait_send())
    each_head(range(4), lambda a, p: send(a, p, p).wait_recv())
    for a in range(4):
        keep(a).wait()


def collect(lists, out, dq, send, own):
    f32, bf = jnp.float32, jnp.bfloat16
    any_spec = pl.BlockSpec(memory_space=pl.ANY)
    tokens = 2 * T // HEADS
    wide = jax.ShapeDtypeStruct((tokens, HEADS * QW), bf)
    thin = jax.ShapeDtypeStruct((tokens, HEADS * D), bf)
    dma = pltpu.SemaphoreType.DMA
    return pl.pallas_call(
        collect_kernel,
        out_shape=(wide, wide, thin, thin),
        in_specs=[pl.BlockSpec(memory_space=pltpu.SMEM)] + [any_spec] * 4,
        out_specs=(any_spec,) * 4,
        scratch_shapes=[
            pltpu.VMEM((2, SIDE, SIDE, T, D), bf),
            pltpu.VMEM((2, SIDE, 2, T, D), bf),
            pltpu.VMEM((2, SIDE, 2, T, D), bf),
            pltpu.VMEM((2, 2, T, D), f32),
            pltpu.VMEM((2, 2 * T, D), bf),
            dma((4, HEADS)), dma((4, HEADS)), dma((2, SIDE)), dma((2, SIDE)),
            dma((2, SIDE)), dma((2, SIDE)), dma((7,)),
        ],
        compiler_params=pltpu.CompilerParams(collective_id=1, has_side_effects=True, vmem_limit_bytes=60 * 2**20),
    )(lists, out, dq, send, own)


def finish_kernel(o_ref, dq_ref, dk_ref, dv_ref, o_res, dq_res, dk_res, dv_res, sem):
    copies = []
    for pair in ((o_ref, o_res), (dq_ref, dq_res)):
        for n in range(4):
            copies.append((pair, pl.ds(n * 32, 32)))
    for pair in ((dk_ref, dk_res), (dv_ref, dv_res)):
        copies.append((pair, pl.ds(0, 128)))
    copies = [pltpu.make_async_copy(pair[0].at[rows], pair[1].at[rows], sem.at[n])
              for n, (pair, rows) in enumerate(copies)]
    for copy in copies:
        copy.start()
    for copy in copies:
        copy.wait()


def finish(arrays):
    any_spec = pl.BlockSpec(memory_space=pl.ANY)
    return pl.pallas_call(
        finish_kernel,
        out_shape=tuple(jax.ShapeDtypeStruct(a.shape, a.dtype) for a in arrays),
        in_specs=[any_spec] * 4,
        out_specs=(any_spec,) * 4,
        scratch_shapes=[pltpu.SemaphoreType.DMA((10,))],
    )(*arrays)


def shards(input_queries, input_keys, input_values, cotangent, block_list, block_count):
    lists = block_list.T
    queries, cot, table = spread(lists, input_queries, input_keys, input_values, cotangent)
    out, dq, send, own = attn(lists, block_count, queries, cot, table)
    return finish(collect(lists, out, dq, send.reshape(SIDE, SIDE, T, 2 * D), own))


def solution(mesh):
    spec = P(("ctx", "head"), None)
    return jax.shard_map(
        shards,
        mesh=mesh,
        in_specs=(spec,) * 4 + (P(), P()),
        out_specs=(spec,) * 4,
        check_vma=False,
    )
```

```python
import jax
import jax.numpy as jnp
from jax import lax
from jax.experimental import pallas as pl
from jax.experimental.pallas import tpu as pltpu
from jax.sharding import PartitionSpec as P

D = 128
T = 512
GROUP = 6
QW = GROUP * D
SIDE = 4
CTX = SIDE * SIDE
HEADS = 8
MOST = 8
SCALE = D**-0.5
LOG2E = 1.4426950408889634
NT = (((1,), (1,)), ((), ()))
MESH = pl.DeviceIdType.MESH


def attn_kernel(lists, counts, q_hbm, cot_hbm, kv_hbm, out_hbm, dq_hbm, send_hbm, own_hbm,
                q, cot, kv, weights, acc, dqa, stat, scaled_t, scaled, out, dq, send, own,
                dscore, qs, kv_sem, in_sem, out_sem, send_sem):
    f32, bf = jnp.float32, jnp.bfloat16
    ctx = lax.axis_index("ctx")

    def owner(b, i):
        return lists[i, 2 * ctx + b] // 2

    def named(b, block_owner):
        hits = jnp.int32(0)
        for n in range(1, MOST):
            hits += (owner(b, n) == block_owner).astype(jnp.int32)
        return hits > 0

    def rows(b):
        return pl.ds(b * T, T)

    def fetch(b, i):
        slot = jnp.where(i == 0, CTX + b, owner(b, i))
        return pltpu.make_async_copy(kv_hbm.at[slot], kv.at[b * MOST + i], kv_sem.at[b * MOST + i])

    def load(b, a):
        source, place = ((q_hbm, q), (cot_hbm, cot))[a]
        return pltpu.make_async_copy(source.at[rows(b)], place.at[rows(b)], in_sem.at[b, a])

    def store(b, a):
        source, place = ((out, out_hbm), (dq, dq_hbm))[a]
        return pltpu.make_async_copy(source.at[rows(b)], place.at[rows(b)], out_sem.at[b, a])

    def store_own(b):
        return pltpu.make_async_copy(own.at[:, b], own_hbm.at[:, b], out_sem.at[b, 2])

    def store_send(d):
        return pltpu.make_async_copy(send.at[d], send_hbm.at[d], send_sem.at[d])

    def each_live(b, act, start=0):
        def one(i, _):
            act(i)
            return 0
        lax.fori_loop(start, counts[2 * ctx + b], one, 0)

    for b in range(2):
        load(b, 0).start()
        each_live(b, lambda i: fetch(b, i).start())
        load(b, 1).start()

    for b in range(2):
        lo = b * T

        def score(i, j):
            return lax.dot_general(kv[b * MOST + i, :, :D], q[lo:lo + T, j * D:(j + 1) * D], NT,
                                   preferred_element_type=f32)

        def top(i):
            for j in range(GROUP):
                best = jnp.max(score(i, j), axis=0, keepdims=True) * (SCALE * LOG2E)
                stat[0, j:j + 1] = jnp.maximum(stat[0, j:j + 1], best)

        def attend(i, shifted):
            values_t = kv[b * MOST + i, :, D:].T
            for j in range(GROUP):
                level = score(i, j) * (SCALE * LOG2E)
                if shifted:
                    level = level - stat[0, j:j + 1]
                weight = jnp.exp2(level)
                stat[1, j:j + 1] += jnp.sum(weight, axis=0, keepdims=True)
                weights[i, :, j * T:(j + 1) * T] = weight.astype(bf)
            for j in range(GROUP):
                acc[j] += jnp.dot(values_t, weights[i, :, j * T:(j + 1) * T], preferred_element_type=f32)

        def clear():
            acc[...] = jnp.zeros_like(acc)
            stat[1] = jnp.zeros((8, T), f32)

        def attend_first(i):
            fetch(b, i).wait()
            attend(i, False)

        load(b, 0).wait()
        clear()
        each_live(b, attend_first)
        sums = stat[1, :GROUP]
        safe = jnp.logical_and(jnp.min(sums) > 2.0**-60, jnp.max(sums) < 2.0**60)

        @pl.when(jnp.logical_not(safe))
        def _():
            stat[0] = jnp.full((8, T), -1e30, f32)
            each_live(b, top)
            clear()
            each_live(b, lambda i: attend(i, True))

        load(b, 1).wait()
        for j in range(GROUP):
            inverse = 1.0 / stat[1, j:j + 1]
            attended = (acc[j] * inverse).astype(bf)
            out[lo:lo + T, j * D:(j + 1) * D] = attended.T
            cot_t = cot[lo:lo + T, j * D:(j + 1) * D].T.astype(f32)
            stat[2, j:j + 1] = jnp.sum(attended.astype(f32) * cot_t, axis=0, keepdims=True) * inverse
            part = (cot_t * inverse).astype(bf)
            scaled_t[j] = part
            scaled[j] = part.T
        store(b, 0).start()
        dqa[...] = jnp.zeros_like(dqa)
        for j in range(GROUP):
            qs[j * T:(j + 1) * T] = q[lo:lo + T, j * D:(j + 1) * D]

        def back(i):
            keys = kv[b * MOST + i, :, :D]
            values = kv[b * MOST + i, :, D:]
            keys_t = keys.T
            dk = jnp.zeros((T, D), f32)
            dv = jnp.zeros((T, D), f32)
            for j in range(GROUP):
                change = jnp.dot(values, scaled_t[j], preferred_element_type=f32) - stat[2, j:j + 1]
                weight = weights[i, :, j * T:(j + 1) * T]
                dscore[:, j * T:(j + 1) * T] = (weight.astype(f32) * change).astype(bf)
            for j in range(GROUP):
                dqa[j] += jnp.dot(keys_t, dscore[:, j * T:(j + 1) * T], preferred_element_type=f32)
            dv = jnp.dot(weights[i], scaled[...].reshape(GROUP * T, D), preferred_element_type=f32)
            dk = jnp.dot(dscore[...], qs[...], preferred_element_type=f32)
            dk = dk * SCALE
            d = owner(b, i)
            other = named(1 - b, d)

            @pl.when(i == 0)
            def _():
                own[0, b] = dk
                own[1, b] = dv

            if b == 0:
                @pl.when(i > 0)
                def _():
                    send[d, :, :D] = dk.astype(bf)
                    send[d, :, D:] = dv.astype(bf)

                @pl.when(jnp.logical_and(i > 0, jnp.logical_not(other)))
                def _():
                    store_send(d).start()
            else:
                @pl.when(jnp.logical_and(i > 0, jnp.logical_not(other)))
                def _():
                    send[d, :, :D] = dk.astype(bf)
                    send[d, :, D:] = dv.astype(bf)

                @pl.when(jnp.logical_and(i > 0, other))
                def _():
                    send[d, :, :D] = (send[d, :, :D].astype(f32) + dk).astype(bf)
                    send[d, :, D:] = (send[d, :, D:].astype(f32) + dv).astype(bf)

                @pl.when(i > 0)
                def _():
                    store_send(d).start()

        each_live(b, back)
        store_own(b).start()
        for j in range(GROUP):
            dq[lo:lo + T, j * D:(j + 1) * D] = (dqa[j] * SCALE).astype(bf).T
        store(b, 1).start()

    def end_first(i):
        d = owner(0, i)

        @pl.when(jnp.logical_not(named(1, d)))
        def _():
            store_send(d).wait()

    each_live(0, end_first, 1)
    each_live(1, lambda i: store_send(owner(1, i)).wait(), 1)
    for b in range(2):
        store(b, 0).wait()
        store(b, 1).wait()
        store_own(b).wait()


def attn(lists, counts, q, cot, kv):
    f32, bf = jnp.float32, jnp.bfloat16
    any_spec = pl.BlockSpec(memory_space=pl.ANY)
    dma = pltpu.SemaphoreType.DMA
    return pl.pallas_call(
        attn_kernel,
        out_shape=(jax.ShapeDtypeStruct((2 * T, QW), bf), jax.ShapeDtypeStruct((2 * T, QW), bf),
                   jax.ShapeDtypeStruct((CTX, T, 2 * D), bf), jax.ShapeDtypeStruct((2, 2, T, D), f32)),
        in_specs=[pl.BlockSpec(memory_space=pltpu.SMEM)] * 2 + [any_spec] * 3,
        out_specs=(any_spec,) * 4,
        scratch_shapes=[
            pltpu.VMEM((2 * T, QW), bf), pltpu.VMEM((2 * T, QW), bf), pltpu.VMEM((2 * MOST, T, 2 * D), bf),
            pltpu.VMEM((MOST, T, GROUP * T), bf), pltpu.VMEM((GROUP, D, T), f32), pltpu.VMEM((GROUP, D, T), f32),
            pltpu.VMEM((3, 8, T), f32), pltpu.VMEM((GROUP, D, T), bf), pltpu.VMEM((GROUP, T, D), bf),
            pltpu.VMEM((2 * T, QW), bf), pltpu.VMEM((2 * T, QW), bf), pltpu.VMEM((CTX, T, 2 * D), bf),
            pltpu.VMEM((2, 2, T, D), f32),
            pltpu.VMEM((T, GROUP * T), bf), pltpu.VMEM((GROUP * T, D), bf),
            dma((2 * MOST,)), dma((2, 2)), dma((2, 3)), dma((CTX,)),
        ],
        compiler_params=pltpu.CompilerParams(vmem_limit_bytes=62 * 2**20),
    )(lists, counts, q, cot, kv)


def greet(ctx, head):
    barrier = pltpu.get_barrier_semaphore()
    y, x = ctx // SIDE, lax.rem(ctx, SIDE)

    def line(n, _):
        pl.semaphore_signal(barrier, inc=1, device_id=(y * SIDE + lax.rem(x + n, SIDE), head), device_id_type=MESH)
        pl.semaphore_signal(barrier, inc=1, device_id=(lax.rem(y + n, SIDE) * SIDE + x, head), device_id_type=MESH)
        return 0

    def head_peer(n, _):
        pl.semaphore_signal(barrier, inc=1, device_id=(ctx, lax.rem(head + n, HEADS)), device_id_type=MESH)
        return 0

    lax.fori_loop(1, SIDE, line, 0)
    lax.fori_loop(1, HEADS, head_peer, 0)
    pl.semaphore_wait(barrier, 2 * (SIDE - 1) + HEADS - 1)


def cols(index, width):
    return pl.ds(pl.multiple_of(index * width, width), width)


def lists_block(lists, ctx, block):
    hits = jnp.int32(0)
    for b in range(2):
        for i in range(1, MOST):
            hits += (lists[i, 2 * ctx + b] == block).astype(jnp.int32)
    return hits > 0


def spread_kernel(lists, q_ref, k_ref, v_ref, c_ref, qh_ref, ch_ref, table_ref,
                  lines, stage, head_send, head_recv, line_send, line_recv, push_send, push_recv, local_sem, fill_sem):
    ctx, head = lax.axis_index("ctx"), lax.axis_index("head")
    y, x = ctx // SIDE, lax.rem(ctx, SIDE)
    here = (x, y)
    greet(ctx, head)
    tokens = k_ref.shape[0]
    arrays = (
        (k_ref, lambda s: lines.at[0, x, cols(s, tokens)], D),
        (v_ref, lambda s: lines.at[1, y, cols(s, tokens)], D),
        (q_ref, lambda s: qh_ref.at[cols(s, tokens)], QW),
        (c_ref, lambda s: ch_ref.at[cols(s, tokens)], QW),
    )

    def at(kind, along, across):
        return across * SIDE + along if kind == 0 else along * SIDE + across

    def send(a, to, frm):
        ref, place, width = arrays[a]
        return pltpu.make_async_remote_copy(
            ref.at[:, cols(to, width)], place(frm), head_send.at[a, to], head_recv.at[a, frm],
            device_id=(ctx, to), device_id_type=MESH)

    def keep(a):
        ref, place, width = arrays[a]
        return pltpu.make_async_copy(ref.at[:, cols(head, width)], place(head), local_sem.at[a])

    def each_head(arrays_used, act):
        def one(n, _):
            peer = lax.rem(head + n, HEADS)
            for a in arrays_used:
                act(a, peer)
            return 0
        lax.fori_loop(1, HEADS, one, 0)

    for a in range(4):
        keep(a).start()
    each_head((0, 1), lambda a, p: send(a, p, head).start())
    each_head((2, 3), lambda a, p: send(a, p, head).start())
    keep(0).wait()
    keep(1).wait()
    each_head((0, 1), lambda a, p: send(a, p, p).wait_recv())

    def share(kind, to, frm):
        return pltpu.make_async_remote_copy(
            lines.at[kind, frm], lines.at[kind, frm], line_send.at[kind, to], line_recv.at[kind, frm],
            device_id=(at(kind, to, here[1 - kind]), head), device_id_type=MESH)

    def push(kind, to, along, frm):
        source = at(kind, along, frm)
        return pltpu.make_async_remote_copy(
            stage.at[kind, to, along], table_ref.at[source, :, kind * D:(kind + 1) * D],
            push_send.at[kind, to, along], push_recv.at[kind, frm, along],
            device_id=(at(kind, here[kind], to), head), device_id_type=MESH)

    def fill(kind, along):
        mine = here[1 - kind]
        return pltpu.make_async_copy(
            stage.at[kind, mine, along], table_ref.at[at(kind, along, mine), :, kind * D:(kind + 1) * D],
            fill_sem.at[kind, along])

    def own(kind, b):
        return pltpu.make_async_copy(
            lines.at[kind, here[kind], b * T:(b + 1) * T], table_ref.at[CTX + b, :, kind * D:(kind + 1) * D],
            local_sem.at[4 + 2 * kind + b])

    def prepare(kind, to, along):
        source = at(kind, along, here[1 - kind])
        second = lists_block(lists, at(kind, here[kind], to), 2 * source + 1)
        stage[kind, to, along] = jnp.where(second, lines[kind, along, T:], lines[kind, along, :T])

    for n in (1, 3, 2):
        for kind in range(2):
            share(kind, lax.rem(here[kind] + n, SIDE), here[kind]).start()
    for kind in range(2):
        for b in range(2):
            own(kind, b).start()

    def push_all(m, _):
        for kind in range(2):
            along = lax.rem(here[kind] + m, SIDE)

            @pl.when(m > 0)
            def _():
                share(kind, along, along).wait_recv()

            for n in range(1, SIDE):
                to = lax.rem(here[1 - kind] + n, SIDE)
                prepare(kind, to, along)
                push(kind, to, along, here[1 - kind]).start()

            @pl.when(m > 0)
            def _():
                prepare(kind, here[1 - kind], along)
                fill(kind, along).start()
        return 0

    lax.fori_loop(0, SIDE, push_all, 0)

    each_head(range(4), lambda a, p: send(a, p, head).wait_send())
    each_head((2, 3), lambda a, p: send(a, p, p).wait_recv())
    keep(2).wait()
    keep(3).wait()

    def drain(m, _):
        for kind in range(2):
            along = lax.rem(here[kind] + m, SIDE)

            @pl.when(m > 0)
            def _():
                share(kind, along, here[kind]).wait_send()
                fill(kind, along).wait()

            for n in range(1, SIDE):
                peer = lax.rem(here[1 - kind] + n, SIDE)
                push(kind, peer, along, here[1 - kind]).wait_send()
                push(kind, peer, along, peer).wait_recv()
        return 0

    lax.fori_loop(0, SIDE, drain, 0)
    for kind in range(2):
        for b in range(2):
            own(kind, b).wait()


def spread(lists, q, k, v, cot):
    bf = jnp.bfloat16
    any_spec = pl.BlockSpec(memory_space=pl.ANY)
    dma = pltpu.SemaphoreType.DMA
    return pl.pallas_call(
        spread_kernel,
        out_shape=(jax.ShapeDtypeStruct((2 * T, QW), bf), jax.ShapeDtypeStruct((2 * T, QW), bf),
                   jax.ShapeDtypeStruct((CTX + 2, T, 2 * D), bf)),
        in_specs=[pl.BlockSpec(memory_space=pltpu.SMEM)] + [any_spec] * 4,
        out_specs=(any_spec,) * 3,
        scratch_shapes=[
            pltpu.VMEM((2, SIDE, 2 * T, D), bf),
            pltpu.VMEM((2, SIDE, SIDE, T, D), bf),
            dma((4, HEADS)), dma((4, HEADS)), dma((2, SIDE)), dma((2, SIDE)),
            dma((2, SIDE, SIDE)), dma((2, SIDE, SIDE)), dma((8,)), dma((2, SIDE)),
        ],
        compiler_params=pltpu.CompilerParams(collective_id=0, has_side_effects=True, vmem_limit_bytes=60 * 2**20),
    )(lists, q, k, v, cot)


def collect_kernel(lists, out_ref, dq_ref, send_ref, own_ref, o_res, dq_res, dk_res, dv_res,
                   first, sums, second, total, grads,
                   head_send, head_recv, line_send, line_recv, push_send, push_recv, local_sem):
    f32, bf = jnp.float32, jnp.bfloat16
    ctx, head = lax.axis_index("ctx"), lax.axis_index("head")
    y, x = ctx // SIDE, lax.rem(ctx, SIDE)
    here = (x, y)
    greet(ctx, head)
    tokens = o_res.shape[0]
    arrays = (
        (lambda to: out_ref.at[cols(to, tokens)], lambda s: o_res.at[:, cols(s, QW)]),
        (lambda to: dq_ref.at[cols(to, tokens)], lambda s: dq_res.at[:, cols(s, QW)]),
        (lambda to: grads.at[0, cols(to, tokens)], lambda s: dk_res.at[:, cols(s, D)]),
        (lambda to: grads.at[1, cols(to, tokens)], lambda s: dv_res.at[:, cols(s, D)]),
    )

    def at(kind, along, across):
        return across * SIDE + along if kind == 0 else along * SIDE + across

    def part(kind, to):
        if kind == 0:
            return send_ref.at[:, to, :, :D]
        return send_ref.at[to, :, :, D:]

    def share(kind, to, frm):
        return pltpu.make_async_remote_copy(
            part(kind, to), first.at[kind, frm], line_send.at[kind, to], line_recv.at[kind, frm],
            device_id=(at(kind, to, here[1 - kind]), head), device_id_type=MESH)

    def hold(kind):
        return pltpu.make_async_copy(part(kind, here[kind]), first.at[kind, here[kind]], local_sem.at[4 + kind])

    def push(kind, to, frm):
        return pltpu.make_async_remote_copy(
            sums.at[kind, to], second.at[kind, frm], push_send.at[kind, to], push_recv.at[kind, frm],
            device_id=(at(kind, here[kind], to), head), device_id_type=MESH)

    def send(a, to, frm):
        source, place = arrays[a]
        return pltpu.make_async_remote_copy(
            source(to), place(frm), head_send.at[a, to], head_recv.at[a, frm],
            device_id=(ctx, to), device_id_type=MESH)

    def keep(a):
        source, place = arrays[a]
        return pltpu.make_async_copy(source(head), place(head), local_sem.at[a])

    def each_head(arrays_used, act):
        def one(n, _):
            peer = lax.rem(head + n, HEADS)
            for a in arrays_used:
                act(a, peer)
            return 0
        lax.fori_loop(1, HEADS, one, 0)

    for n in (1, 3, 2):
        for kind in range(2):
            share(kind, lax.rem(here[kind] + n, SIDE), here[kind]).start()
    for kind in range(2):
        hold(kind).start()
    each_head((0, 1), lambda a, p: send(a, p, head).start())
    keep(0).start()
    keep(1).start()
    start_total = pltpu.make_async_copy(own_ref, total, local_sem.at[6])
    start_total.start()
    for kind in range(2):
        hold(kind).wait()
        for n in range(1, SIDE):
            peer = lax.rem(here[kind] + n, SIDE)
            share(kind, peer, peer).wait_recv()

    def add_line(n, _):
        for kind in range(2):
            to = lax.rem(here[1 - kind] + n, SIDE)
            target = at(kind, here[kind], to)
            for b in range(2):
                acc = jnp.zeros((T, D), f32)
                for along in range(SIDE):
                    source = at(kind, along, here[1 - kind])
                    take = jnp.logical_and(lists_block(lists, source, 2 * target + b), source != target)
                    acc += jnp.where(take, first[kind, along, to].astype(f32), 0.0)
                sums[kind, to, b] = acc.astype(bf)

            @pl.when(n < SIDE)
            def _():
                push(kind, to, here[1 - kind]).start()
        return 0

    lax.fori_loop(1, SIDE + 1, add_line, 0)
    start_total.wait()
    for kind in range(2):
        for b in range(2):
            total[kind, b] += sums[kind, here[1 - kind], b].astype(f32)
        for n in range(1, SIDE):
            frm = lax.rem(here[1 - kind] + n, SIDE)
            push(kind, frm, frm).wait_recv()
            for b in range(2):
                total[kind, b] += second[kind, frm, b].astype(f32)
        for b in range(2):
            grads[kind, b * T:(b + 1) * T] = total[kind, b].astype(bf)

    each_head((2, 3), lambda a, p: send(a, p, head).start())
    keep(2).start()
    keep(3).start()
    for kind in range(2):
        for n in range(1, SIDE):
            share(kind, lax.rem(here[kind] + n, SIDE), here[kind]).wait_send()
            push(kind, lax.rem(here[1 - kind] + n, SIDE), here[1 - kind]).wait_send()
    each_head(range(4), lambda a, p: send(a, p, head).wait_send())
    each_head(range(4), lambda a, p: send(a, p, p).wait_recv())
    for a in range(4):
        keep(a).wait()


def collect(lists, out, dq, send, own):
    f32, bf = jnp.float32, jnp.bfloat16
    any_spec = pl.BlockSpec(memory_space=pl.ANY)
    tokens = 2 * T // HEADS
    wide = jax.ShapeDtypeStruct((tokens, HEADS * QW), bf)
    thin = jax.ShapeDtypeStruct((tokens, HEADS * D), bf)
    dma = pltpu.SemaphoreType.DMA
    return pl.pallas_call(
        collect_kernel,
        out_shape=(wide, wide, thin, thin),
        in_specs=[pl.BlockSpec(memory_space=pltpu.SMEM)] + [any_spec] * 4,
        out_specs=(any_spec,) * 4,
        scratch_shapes=[
            pltpu.VMEM((2, SIDE, SIDE, T, D), bf),
            pltpu.VMEM((2, SIDE, 2, T, D), bf),
            pltpu.VMEM((2, SIDE, 2, T, D), bf),
            pltpu.VMEM((2, 2, T, D), f32),
            pltpu.VMEM((2, 2 * T, D), bf),
            dma((4, HEADS)), dma((4, HEADS)), dma((2, SIDE)), dma((2, SIDE)),
            dma((2, SIDE)), dma((2, SIDE)), dma((7,)),
        ],
        compiler_params=pltpu.CompilerParams(collective_id=1, has_side_effects=True, vmem_limit_bytes=60 * 2**20),
    )(lists, out, dq, send, own)


def finish_kernel(o_ref, dq_ref, dk_ref, dv_ref, o_res, dq_res, dk_res, dv_res, wide, thin, in_sem, out_sem):
    moves = []
    for n in range(8):
        moves.append(((o_ref, dq_ref)[n % 2], wide.at[n % 2], (o_res, dq_res)[n % 2], pl.ds(n // 2 * 32, 32)))
    for n in range(2):
        moves.append(((dk_ref, dv_ref)[n], thin.at[n], (dk_res, dv_res)[n], pl.ds(0, 128)))
    reads = [pltpu.make_async_copy(source.at[rows], held.at[rows], in_sem.at[n])
             for n, (source, held, _, rows) in enumerate(moves)]
    writes = [pltpu.make_async_copy(held.at[rows], target.at[rows], out_sem.at[n])
              for n, (_, held, target, rows) in enumerate(moves)]
    for read in reads:
        read.start()
    for read, write in zip(reads, writes):
        read.wait()
        write.start()
    for write in writes:
        write.wait()


def finish(arrays):
    any_spec = pl.BlockSpec(memory_space=pl.ANY)
    return pl.pallas_call(
        finish_kernel,
        out_shape=tuple(jax.ShapeDtypeStruct(a.shape, a.dtype) for a in arrays),
        in_specs=[any_spec] * 4,
        out_specs=(any_spec,) * 4,
        scratch_shapes=[pltpu.VMEM((2, 128, HEADS * QW), jnp.bfloat16), pltpu.VMEM((2, 128, HEADS * D), jnp.bfloat16),
                        pltpu.SemaphoreType.DMA((10,)), pltpu.SemaphoreType.DMA((10,))],
        compiler_params=pltpu.CompilerParams(vmem_limit_bytes=60 * 2**20),
    )(*arrays)


def shards(input_queries, input_keys, input_values, cotangent, block_list, block_count):
    lists = block_list.T
    queries, cot, table = spread(lists, input_queries, input_keys, input_values, cotangent)
    out, dq, send, own = attn(lists, block_count, queries, cot, table)
    return finish(collect(lists, out, dq, send.reshape(SIDE, SIDE, T, 2 * D), own))


def solution(mesh):
    spec = P(("ctx", "head"), None)
    return jax.shard_map(
        shards,
        mesh=mesh,
        in_specs=(spec,) * 4 + (P(), P()),
        out_specs=(spec,) * 4,
        check_vma=False,
    )
```

```python
import jax
import jax.numpy as jnp
from jax import lax
from jax.experimental import pallas as pl
from jax.experimental.pallas import tpu as pltpu
from jax.sharding import PartitionSpec as P

D = 128
T = 512
GROUP = 6
QW = GROUP * D
SIDE = 4
CTX = SIDE * SIDE
HEADS = 8
MOST = 8
SCALE = D**-0.5
LOG2E = 1.4426950408889634
NT = (((1,), (1,)), ((), ()))
MESH = pl.DeviceIdType.MESH


def attn_kernel(lists, counts, q_hbm, cot_hbm, kv_hbm, out_hbm, dq_hbm, send_hbm, own_hbm,
                q, cot, kv, weights, acc, dqa, stat, scaled_t, scaled, out, dq, send, own,
                dscore, qs, kv_sem, in_sem, out_sem, send_sem):
    f32, bf = jnp.float32, jnp.bfloat16
    ctx = lax.axis_index("ctx")

    def owner(b, i):
        return lists[i, 2 * ctx + b] // 2

    def named(b, block_owner):
        hits = jnp.int32(0)
        for n in range(1, MOST):
            hits += (owner(b, n) == block_owner).astype(jnp.int32)
        return hits > 0

    def rows(b):
        return pl.ds(b * T, T)

    def fetch(b, i):
        slot = jnp.where(i == 0, CTX + b, owner(b, i))
        return pltpu.make_async_copy(kv_hbm.at[slot], kv.at[b * MOST + i], kv_sem.at[b * MOST + i])

    def load(b, a):
        source, place = ((q_hbm, q), (cot_hbm, cot))[a]
        return pltpu.make_async_copy(source.at[rows(b)], place.at[rows(b)], in_sem.at[b, a])

    def store(b, a):
        source, place = ((out, out_hbm), (dq, dq_hbm))[a]
        return pltpu.make_async_copy(source.at[rows(b)], place.at[rows(b)], out_sem.at[b, a])

    def store_own(b):
        return pltpu.make_async_copy(own.at[:, b], own_hbm.at[:, b], out_sem.at[b, 2])

    def store_send(d):
        return pltpu.make_async_copy(send.at[d], send_hbm.at[d], send_sem.at[d])

    def each_live(b, act, start=0):
        def one(i, _):
            act(i)
            return 0
        lax.fori_loop(start, counts[2 * ctx + b], one, 0)

    for b in range(2):
        load(b, 0).start()
        each_live(b, lambda i: fetch(b, i).start())
        load(b, 1).start()

    for b in range(2):
        lo = b * T

        def score(i, j):
            return lax.dot_general(kv[b * MOST + i, :, :D], q[lo:lo + T, j * D:(j + 1) * D], NT,
                                   preferred_element_type=f32)

        def top(i):
            for j in range(GROUP):
                best = jnp.max(score(i, j), axis=0, keepdims=True) * (SCALE * LOG2E)
                stat[0, j:j + 1] = jnp.maximum(stat[0, j:j + 1], best)

        def attend(i, shifted):
            values_t = kv[b * MOST + i, :, D:].T
            for j in range(GROUP):
                level = score(i, j) * (SCALE * LOG2E)
                if shifted:
                    level = level - stat[0, j:j + 1]
                weight = jnp.exp2(level)
                stat[1, j:j + 1] += jnp.sum(weight, axis=0, keepdims=True)
                weights[i, :, j * T:(j + 1) * T] = weight.astype(bf)
            for j in range(GROUP):
                acc[j] += jnp.dot(values_t, weights[i, :, j * T:(j + 1) * T], preferred_element_type=f32)

        def clear():
            acc[...] = jnp.zeros_like(acc)
            stat[1] = jnp.zeros((8, T), f32)

        def attend_first(i):
            fetch(b, i).wait()
            attend(i, False)

        load(b, 0).wait()
        clear()
        each_live(b, attend_first)
        sums = stat[1, :GROUP]
        safe = jnp.logical_and(jnp.min(sums) > 2.0**-60, jnp.max(sums) < 2.0**60)

        @pl.when(jnp.logical_not(safe))
        def _():
            stat[0] = jnp.full((8, T), -1e30, f32)
            each_live(b, top)
            clear()
            each_live(b, lambda i: attend(i, True))

        load(b, 1).wait()
        for j in range(GROUP):
            inverse = 1.0 / stat[1, j:j + 1]
            attended = (acc[j] * inverse).astype(bf)
            out[lo:lo + T, j * D:(j + 1) * D] = attended.T
            cot_t = cot[lo:lo + T, j * D:(j + 1) * D].T.astype(f32)
            stat[2, j:j + 1] = jnp.sum(attended.astype(f32) * cot_t, axis=0, keepdims=True) * inverse
            part = (cot_t * inverse).astype(bf)
            scaled_t[j] = part
            scaled[j] = part.T
        store(b, 0).start()
        dqa[...] = jnp.zeros_like(dqa)
        for j in range(GROUP):
            qs[j * T:(j + 1) * T] = q[lo:lo + T, j * D:(j + 1) * D]

        def back(i):
            keys = kv[b * MOST + i, :, :D]
            values = kv[b * MOST + i, :, D:]
            keys_t = keys.T
            dk = jnp.zeros((T, D), f32)
            dv = jnp.zeros((T, D), f32)
            for j in range(GROUP):
                change = jnp.dot(values, scaled_t[j], preferred_element_type=f32) - stat[2, j:j + 1]
                weight = weights[i, :, j * T:(j + 1) * T]
                dscore[:, j * T:(j + 1) * T] = (weight.astype(f32) * change).astype(bf)
            for j in range(GROUP):
                dqa[j] += jnp.dot(keys_t, dscore[:, j * T:(j + 1) * T], preferred_element_type=f32)
            dv = jnp.dot(weights[i], scaled[...].reshape(GROUP * T, D), preferred_element_type=f32)
            dk = jnp.dot(dscore[...], qs[...], preferred_element_type=f32)
            dk = dk * SCALE
            d = owner(b, i)
            other = named(1 - b, d)

            @pl.when(i == 0)
            def _():
                own[0, b] = dk
                own[1, b] = dv
                store_own(b).start()

            if b == 0:
                @pl.when(i > 0)
                def _():
                    send[d, :, :D] = dk.astype(bf)
                    send[d, :, D:] = dv.astype(bf)

                @pl.when(jnp.logical_and(i > 0, jnp.logical_not(other)))
                def _():
                    store_send(d).start()
            else:
                @pl.when(jnp.logical_and(i > 0, jnp.logical_not(other)))
                def _():
                    send[d, :, :D] = dk.astype(bf)
                    send[d, :, D:] = dv.astype(bf)

                @pl.when(jnp.logical_and(i > 0, other))
                def _():
                    send[d, :, :D] = (send[d, :, :D].astype(f32) + dk).astype(bf)
                    send[d, :, D:] = (send[d, :, D:].astype(f32) + dv).astype(bf)

                @pl.when(i > 0)
                def _():
                    store_send(d).start()

        each_live(b, back)
        for j in range(GROUP):
            dq[lo:lo + T, j * D:(j + 1) * D] = (dqa[j] * SCALE).astype(bf).T
        store(b, 1).start()

    def end_first(i):
        d = owner(0, i)

        @pl.when(jnp.logical_not(named(1, d)))
        def _():
            store_send(d).wait()

    each_live(0, end_first, 1)
    each_live(1, lambda i: store_send(owner(1, i)).wait(), 1)
    for b in range(2):
        store(b, 0).wait()
        store(b, 1).wait()
        store_own(b).wait()


def attn(lists, counts, q, cot, kv):
    f32, bf = jnp.float32, jnp.bfloat16
    any_spec = pl.BlockSpec(memory_space=pl.ANY)
    dma = pltpu.SemaphoreType.DMA
    return pl.pallas_call(
        attn_kernel,
        out_shape=(jax.ShapeDtypeStruct((2 * T, QW), bf), jax.ShapeDtypeStruct((2 * T, QW), bf),
                   jax.ShapeDtypeStruct((CTX, T, 2 * D), bf), jax.ShapeDtypeStruct((2, 2, T, D), f32)),
        in_specs=[pl.BlockSpec(memory_space=pltpu.SMEM)] * 2 + [any_spec] * 3,
        out_specs=(any_spec,) * 4,
        scratch_shapes=[
            pltpu.VMEM((2 * T, QW), bf), pltpu.VMEM((2 * T, QW), bf), pltpu.VMEM((2 * MOST, T, 2 * D), bf),
            pltpu.VMEM((MOST, T, GROUP * T), bf), pltpu.VMEM((GROUP, D, T), f32), pltpu.VMEM((GROUP, D, T), f32),
            pltpu.VMEM((3, 8, T), f32), pltpu.VMEM((GROUP, D, T), bf), pltpu.VMEM((GROUP, T, D), bf),
            pltpu.VMEM((2 * T, QW), bf), pltpu.VMEM((2 * T, QW), bf), pltpu.VMEM((CTX, T, 2 * D), bf),
            pltpu.VMEM((2, 2, T, D), f32),
            pltpu.VMEM((T, GROUP * T), bf), pltpu.VMEM((GROUP * T, D), bf),
            dma((2 * MOST,)), dma((2, 2)), dma((2, 3)), dma((CTX,)),
        ],
        compiler_params=pltpu.CompilerParams(vmem_limit_bytes=62 * 2**20),
    )(lists, counts, q, cot, kv)


def greet(ctx, head):
    barrier = pltpu.get_barrier_semaphore()
    y, x = ctx // SIDE, lax.rem(ctx, SIDE)

    def line(n, _):
        pl.semaphore_signal(barrier, inc=1, device_id=(y * SIDE + lax.rem(x + n, SIDE), head), device_id_type=MESH)
        pl.semaphore_signal(barrier, inc=1, device_id=(lax.rem(y + n, SIDE) * SIDE + x, head), device_id_type=MESH)
        return 0

    def head_peer(n, _):
        pl.semaphore_signal(barrier, inc=1, device_id=(ctx, lax.rem(head + n, HEADS)), device_id_type=MESH)
        return 0

    lax.fori_loop(1, SIDE, line, 0)
    lax.fori_loop(1, HEADS, head_peer, 0)
    pl.semaphore_wait(barrier, 2 * (SIDE - 1) + HEADS - 1)


def cols(index, width):
    return pl.ds(pl.multiple_of(index * width, width), width)


def lists_block(lists, ctx, block):
    hits = jnp.int32(0)
    for b in range(2):
        for i in range(1, MOST):
            hits += (lists[i, 2 * ctx + b] == block).astype(jnp.int32)
    return hits > 0


def spread_kernel(lists, q_ref, k_ref, v_ref, c_ref, qh_ref, ch_ref, table_ref,
                  lines, stage, flags, head_send, head_recv, line_send, line_recv, push_send, push_recv,
                  local_sem, fill_sem):
    ctx, head = lax.axis_index("ctx"), lax.axis_index("head")
    y, x = ctx // SIDE, lax.rem(ctx, SIDE)
    here = (x, y)
    greet(ctx, head)
    tokens = k_ref.shape[0]
    arrays = (
        (k_ref, lambda s: lines.at[0, x, cols(s, tokens)], D),
        (v_ref, lambda s: lines.at[1, y, cols(s, tokens)], D),
        (q_ref, lambda s: qh_ref.at[cols(s, tokens)], QW),
        (c_ref, lambda s: ch_ref.at[cols(s, tokens)], QW),
    )

    def at(kind, along, across):
        return across * SIDE + along if kind == 0 else along * SIDE + across

    def send(a, to, frm):
        ref, place, width = arrays[a]
        return pltpu.make_async_remote_copy(
            ref.at[:, cols(to, width)], place(frm), head_send.at[a, to], head_recv.at[a, frm],
            device_id=(ctx, to), device_id_type=MESH)

    def keep(a):
        ref, place, width = arrays[a]
        return pltpu.make_async_copy(ref.at[:, cols(head, width)], place(head), local_sem.at[a])

    def each_head(arrays_used, act):
        def one(n, _):
            peer = lax.rem(head + 3 * n, HEADS)
            for a in arrays_used:
                act(a, peer)
            return 0
        lax.fori_loop(1, HEADS, one, 0)

    for a in range(4):
        keep(a).start()
    each_head((0, 1), lambda a, p: send(a, p, head).start())
    each_head((2, 3), lambda a, p: send(a, p, head).start())
    for kind in range(2):
        def mark(e, _):
            to, along = e // SIDE, lax.rem(e, SIDE)
            source = at(kind, along, here[1 - kind])
            hit = lists_block(lists, at(kind, here[kind], to), 2 * source + 1)
            flags[kind * CTX + e] = hit.astype(jnp.int32)
            return 0

        lax.fori_loop(0, CTX, mark, 0)
    def share(kind, to, frm, block):
        place = lines.at[kind, frm, cols(block, T)]
        return pltpu.make_async_remote_copy(
            place, place, line_send.at[kind, to, block], line_recv.at[kind, frm, block],
            device_id=(at(kind, to, here[1 - kind]), head), device_id_type=MESH)

    def push(kind, to, along, frm):
        source = at(kind, along, frm)
        return pltpu.make_async_remote_copy(
            stage.at[kind, to, along], table_ref.at[source, :, kind * D:(kind + 1) * D],
            push_send.at[kind, to, along], push_recv.at[kind, frm, along],
            device_id=(at(kind, here[kind], to), head), device_id_type=MESH)

    def fill(kind, along):
        mine = here[1 - kind]
        return pltpu.make_async_copy(
            stage.at[kind, mine, along], table_ref.at[at(kind, along, mine), :, kind * D:(kind + 1) * D],
            fill_sem.at[kind, along])

    def own(kind, b):
        return pltpu.make_async_copy(
            lines.at[kind, here[kind], b * T:(b + 1) * T], table_ref.at[CTX + b, :, kind * D:(kind + 1) * D],
            local_sem.at[4 + 2 * kind + b])

    def prepare(kind, to, along):
        second = flags[kind * CTX + to * SIDE + along] > 0
        stage[kind, to, along] = jnp.where(second, lines[kind, along, T:], lines[kind, along, :T])

    keep(0).wait()
    keep(1).wait()
    for half in range(2):
        block = lax.rem(head // SIDE + half, 2)

        def take_kv(n, _):
            frm = block * SIDE + lax.rem(head + n, SIDE)
            send(0, frm, frm).wait_recv()
            send(1, frm, frm).wait_recv()
            return 0

        lax.fori_loop(1 - half, SIDE, take_kv, 0)
        for n in (1, 3, 2):
            for kind in range(2):
                share(kind, lax.rem(here[kind] + n, SIDE), here[kind], block).start()
    for kind in range(2):
        for b in range(2):
            own(kind, b).start()

    def push_all(m, _):
        for kind in range(2):
            along = lax.rem(here[kind] + m + m // 2 - 2 * (m // 3), SIDE)

            @pl.when(m > 0)
            def _():
                share(kind, along, along, 0).wait_recv()
                share(kind, along, along, 1).wait_recv()

            for n in (2, 1, 3):
                to = lax.rem(here[1 - kind] + n, SIDE)
                prepare(kind, to, along)
                push(kind, to, along, here[1 - kind]).start()

            @pl.when(m > 0)
            def _():
                prepare(kind, here[1 - kind], along)
                fill(kind, along).start()
        return 0

    lax.fori_loop(0, SIDE, push_all, 0)

    each_head(range(4), lambda a, p: send(a, p, head).wait_send())
    each_head((2, 3), lambda a, p: send(a, p, p).wait_recv())
    keep(2).wait()
    keep(3).wait()

    def drain(m, _):
        for kind in range(2):
            along = lax.rem(here[kind] + m, SIDE)

            @pl.when(m > 0)
            def _():
                share(kind, along, here[kind], 0).wait_send()
                share(kind, along, here[kind], 1).wait_send()
                fill(kind, along).wait()

            for n in range(1, SIDE):
                peer = lax.rem(here[1 - kind] + n, SIDE)
                push(kind, peer, along, here[1 - kind]).wait_send()
                push(kind, peer, along, peer).wait_recv()
        return 0

    lax.fori_loop(0, SIDE, drain, 0)
    for kind in range(2):
        for b in range(2):
            own(kind, b).wait()


def spread(lists, q, k, v, cot):
    bf = jnp.bfloat16
    any_spec = pl.BlockSpec(memory_space=pl.ANY)
    dma = pltpu.SemaphoreType.DMA
    return pl.pallas_call(
        spread_kernel,
        out_shape=(jax.ShapeDtypeStruct((2 * T, QW), bf), jax.ShapeDtypeStruct((2 * T, QW), bf),
                   jax.ShapeDtypeStruct((CTX + 2, T, 2 * D), bf)),
        in_specs=[pl.BlockSpec(memory_space=pltpu.SMEM)] + [any_spec] * 4,
        out_specs=(any_spec,) * 3,
        scratch_shapes=[
            pltpu.VMEM((2, SIDE, 2 * T, D), bf),
            pltpu.VMEM((2, SIDE, SIDE, T, D), bf),
            pltpu.SMEM((2 * CTX,), jnp.int32),
            dma((4, HEADS)), dma((4, HEADS)), dma((2, SIDE, 2)), dma((2, SIDE, 2)),
            dma((2, SIDE, SIDE)), dma((2, SIDE, SIDE)), dma((8,)), dma((2, SIDE)),
        ],
        compiler_params=pltpu.CompilerParams(collective_id=0, has_side_effects=True, vmem_limit_bytes=60 * 2**20),
    )(lists, q, k, v, cot)


def collect_kernel(lists, out_ref, dq_ref, send_ref, own_ref, o_res, dq_res, dk_res, dv_res,
                   first, sums, second, total, grads, flags,
                   head_send, head_recv, line_send, line_recv, push_send, push_recv, local_sem):
    f32, bf = jnp.float32, jnp.bfloat16
    ctx, head = lax.axis_index("ctx"), lax.axis_index("head")
    y, x = ctx // SIDE, lax.rem(ctx, SIDE)
    here = (x, y)
    greet(ctx, head)
    tokens = o_res.shape[0]
    arrays = (
        (lambda to: out_ref.at[cols(to, tokens)], lambda s: o_res.at[:, cols(s, QW)]),
        (lambda to: dq_ref.at[cols(to, tokens)], lambda s: dq_res.at[:, cols(s, QW)]),
        (lambda to: grads.at[0, cols(to, tokens)], lambda s: dk_res.at[:, cols(s, D)]),
        (lambda to: grads.at[1, cols(to, tokens)], lambda s: dv_res.at[:, cols(s, D)]),
    )

    def at(kind, along, across):
        return across * SIDE + along if kind == 0 else along * SIDE + across

    def part(kind, to):
        if kind == 0:
            return send_ref.at[:, to, :, :D]
        return send_ref.at[to, :, :, D:]

    def share(kind, to, frm, piece):
        source = send_ref.at[piece, to, :, :D] if kind == 0 else send_ref.at[to, piece, :, D:]
        return pltpu.make_async_remote_copy(
            source, first.at[kind, frm, piece], line_send.at[kind, to, piece], line_recv.at[kind, frm, piece],
            device_id=(at(kind, to, here[1 - kind]), head), device_id_type=MESH)

    def hold(kind):
        return pltpu.make_async_copy(part(kind, here[kind]), first.at[kind, here[kind]], local_sem.at[4 + kind])

    def push(kind, to, frm):
        return pltpu.make_async_remote_copy(
            sums.at[kind, to], second.at[kind, frm], push_send.at[kind, to], push_recv.at[kind, frm],
            device_id=(at(kind, here[kind], to), head), device_id_type=MESH)

    def send(a, to, frm):
        source, place = arrays[a]
        return pltpu.make_async_remote_copy(
            source(to), place(frm), head_send.at[a, to], head_recv.at[a, frm],
            device_id=(ctx, to), device_id_type=MESH)

    def keep(a):
        source, place = arrays[a]
        return pltpu.make_async_copy(source(head), place(head), local_sem.at[a])

    def each_head(arrays_used, act):
        def one(n, _):
            peer = lax.rem(head + 3 * n, HEADS)
            for a in arrays_used:
                act(a, peer)
            return 0
        lax.fori_loop(1, HEADS, one, 0)

    def start_pieces(m, _):
        for n in (2, 1, 3):
            for kind in range(2):
                piece = lax.rem(here[1 - kind] + m, SIDE)
                share(kind, lax.rem(here[kind] + n, SIDE), here[kind], piece).start()
        return 0

    lax.fori_loop(1, SIDE + 1, start_pieces, 0)
    for kind in range(2):
        hold(kind).start()
    each_head((0, 1), lambda a, p: send(a, p, head).start())
    keep(0).start()
    keep(1).start()
    start_total = pltpu.make_async_copy(own_ref, total, local_sem.at[6])
    start_total.start()
    for kind in range(2):
        def mark(e, _):
            to, b, along = e // (2 * SIDE), lax.rem(e // SIDE, 2), lax.rem(e, SIDE)
            target = at(kind, here[kind], to)
            source = at(kind, along, here[1 - kind])
            hit = jnp.logical_and(lists_block(lists, source, 2 * target + b), source != target)
            flags[kind * 2 * CTX + e] = hit.astype(jnp.int32)
            return 0

        lax.fori_loop(0, 2 * CTX, mark, 0)
    for kind in range(2):
        hold(kind).wait()

    def add_line(n, _):
        for kind in range(2):
            to = lax.rem(here[1 - kind] + n, SIDE)
            for m in range(1, SIDE):
                peer = lax.rem(here[kind] + m, SIDE)
                share(kind, peer, peer, to).wait_recv()
            for b in range(2):
                acc = jnp.zeros((T, D), f32)
                for along in range(SIDE):
                    take = flags[kind * 2 * CTX + (2 * to + b) * SIDE + along] > 0
                    acc += jnp.where(take, first[kind, along, to].astype(f32), 0.0)
                sums[kind, to, b] = acc.astype(bf)

            @pl.when(n < SIDE)
            def _():
                push(kind, to, here[1 - kind]).start()
        return 0

    lax.fori_loop(1, SIDE + 1, add_line, 0)
    start_total.wait()
    for kind in range(2):
        for b in range(2):
            total[kind, b] += sums[kind, here[1 - kind], b].astype(f32)
        for n in range(1, SIDE):
            frm = lax.rem(here[1 - kind] + n, SIDE)
            push(kind, frm, frm).wait_recv()
            for b in range(2):
                total[kind, b] += second[kind, frm, b].astype(f32)
        for b in range(2):
            grads[kind, b * T:(b + 1) * T] = total[kind, b].astype(bf)
        each_head((2 + kind,), lambda a, p: send(a, p, head).start())
        keep(2 + kind).start()

    for kind in range(2):
        for n in range(1, SIDE):
            for piece in range(SIDE):
                share(kind, lax.rem(here[kind] + n, SIDE), here[kind], piece).wait_send()
            push(kind, lax.rem(here[1 - kind] + n, SIDE), here[1 - kind]).wait_send()
    each_head(range(4), lambda a, p: send(a, p, head).wait_send())
    each_head(range(4), lambda a, p: send(a, p, p).wait_recv())
    for a in range(4):
        keep(a).wait()


def collect(lists, out, dq, send, own):
    f32, bf = jnp.float32, jnp.bfloat16
    any_spec = pl.BlockSpec(memory_space=pl.ANY)
    tokens = 2 * T // HEADS
    wide = jax.ShapeDtypeStruct((tokens, HEADS * QW), bf)
    thin = jax.ShapeDtypeStruct((tokens, HEADS * D), bf)
    dma = pltpu.SemaphoreType.DMA
    return pl.pallas_call(
        collect_kernel,
        out_shape=(wide, wide, thin, thin),
        in_specs=[pl.BlockSpec(memory_space=pltpu.SMEM)] + [any_spec] * 4,
        out_specs=(any_spec,) * 4,
        scratch_shapes=[
            pltpu.VMEM((2, SIDE, SIDE, T, D), bf),
            pltpu.VMEM((2, SIDE, 2, T, D), bf),
            pltpu.VMEM((2, SIDE, 2, T, D), bf),
            pltpu.VMEM((2, 2, T, D), f32),
            pltpu.VMEM((2, 2 * T, D), bf),
            pltpu.SMEM((4 * CTX,), jnp.int32),
            dma((4, HEADS)), dma((4, HEADS)), dma((2, SIDE, SIDE)), dma((2, SIDE, SIDE)),
            dma((2, SIDE)), dma((2, SIDE)), dma((7,)),
        ],
        compiler_params=pltpu.CompilerParams(collective_id=1, has_side_effects=True, vmem_limit_bytes=60 * 2**20),
    )(lists, out, dq, send, own)


def finish_kernel(o_ref, dq_ref, dk_ref, dv_ref, o_res, dq_res, dk_res, dv_res, wide, thin, in_sem, out_sem):
    moves = []
    for n in range(8):
        moves.append(((o_ref, dq_ref)[n % 2], wide.at[n % 2], (o_res, dq_res)[n % 2], pl.ds(n // 2 * 32, 32)))
    for n in range(2):
        moves.append(((dk_ref, dv_ref)[n], thin.at[n], (dk_res, dv_res)[n], pl.ds(0, 128)))
    reads = [pltpu.make_async_copy(source.at[rows], held.at[rows], in_sem.at[n])
             for n, (source, held, _, rows) in enumerate(moves)]
    writes = [pltpu.make_async_copy(held.at[rows], target.at[rows], out_sem.at[n])
              for n, (_, held, target, rows) in enumerate(moves)]
    for read in reads:
        read.start()
    for read, write in zip(reads, writes):
        read.wait()
        write.start()
    for write in writes:
        write.wait()


def finish(arrays):
    any_spec = pl.BlockSpec(memory_space=pl.ANY)
    return pl.pallas_call(
        finish_kernel,
        out_shape=tuple(jax.ShapeDtypeStruct(a.shape, a.dtype) for a in arrays),
        in_specs=[any_spec] * 4,
        out_specs=(any_spec,) * 4,
        scratch_shapes=[pltpu.VMEM((2, 128, HEADS * QW), jnp.bfloat16), pltpu.VMEM((2, 128, HEADS * D), jnp.bfloat16),
                        pltpu.SemaphoreType.DMA((10,)), pltpu.SemaphoreType.DMA((10,))],
        compiler_params=pltpu.CompilerParams(vmem_limit_bytes=60 * 2**20),
    )(*arrays)


def shards(input_queries, input_keys, input_values, cotangent, block_list, block_count):
    lists = block_list.T
    queries, cot, table = spread(lists, input_queries, input_keys, input_values, cotangent)
    out, dq, send, own = attn(lists, block_count, queries, cot, table)
    return finish(collect(lists, out, dq, send.reshape(SIDE, SIDE, T, 2 * D), own))


def solution(mesh):
    spec = P(("ctx", "head"), None)
    return jax.shard_map(
        shards,
        mesh=mesh,
        in_specs=(spec,) * 4 + (P(), P()),
        out_specs=(spec,) * 4,
        check_vma=False,
    )
```
